256 devices in a mesh: section: 4 (over y), tensor: 16 (over z_lo, x, core), dp: 4 (over z_hi).
Axes of the slice: x: 4, y: 4, z: 8 (z_hi: 4, z_lo: 2; z = z_hi * 2 + z_lo), core: 2. Of those that a mesh axis runs over, the one named last changes fastest.
Arguments:
- grad_out: bfloat16 [4, 4, 256, 6144], P('section', 'dp', 'tensor'), may hold values from -6 to 6
- saved_input: bfloat16 [4, 4, 256, 6144], P('section', 'dp', 'tensor'), may hold values from -6 to 6
- pre_act: bfloat16 [4, 4, 256, 12288], P('section', 'dp', None, 'tensor'), may hold values from -8 to 8
- error: float32 [4, 4, 256, 6144], P('section', 'dp', 'tensor'), may hold values from -3 to 3
- w_up: bfloat16 [4, 6144, 12288], P('section', 'dp', 'tensor'), may hold values from -0.078125 to 0.078125
- w_down: bfloat16 [4, 12288, 6144], P('section', 'tensor', 'dp'), may hold values from -0.0546875 to 0.0546875
- q_init: bfloat16 [4, 6144, 128], P('section'), may hold values from -0.078125 to 0.078125
Outputs:
- grad_up: bfloat16 [4, 6144, 12288], P('section', 'dp', 'tensor')
- grad_down: bfloat16 [4, 12288, 6144], P('section', 'tensor', 'dp')
- new_error: float32 [4, 4, 256, 6144], P('section', 'dp', 'tensor')
- received: bfloat16 [4, 4, 256, 6144], P('section', 'dp', 'tensor')
The draws below stay inside these ranges and needn't reach their ends.
All inputs are finite; a program needn't handle non-finite values.
Results may differ from the reference program's by a relative error of at most 0.03.
Values may be sent and summed in bfloat16 or wider, within the bound.
A program may use at most 128 MiB of HBM per device.

```python
import jax
import jax.numpy as jnp
from jax import lax

D = 6144
HID = 12288
RANK = 128
TOK_G = 256
SECTIONS = 4
REPLICAS = 4
N_SECTION = 4
N_DP = 4


def shard_levels(own_key, dims, shards, smallest, top_value):
    def one(axis_at, shards_of):
        draws = jax.random.uniform(jax.random.fold_in(jax.random.fold_in(own_key, 6), axis_at), (shards_of,), jnp.float32, smallest / len(shards), top_value / len(shards))
        return jnp.repeat(jnp.exp(draws), dims[axis_at] // shards_of).reshape((-1,) + (1,) * (len(dims) - axis_at - 1))

    factor_of = one(*shards[0])
    for cut in shards[1:]:
        factor_of = factor_of * one(*cut)
    return factor_of


def centred(rng, extent, deviation, bound, shards=(), kind=jnp.bfloat16):
    entries = jax.random.normal(rng, extent, jnp.float32) * deviation
    if len(shards) > 0:
        entries = shard_levels(rng, extent, shards, -0.22, 0.18) * entries
    return jnp.clip(entries, min=-bound, max=bound).astype(kind)


def setup_inputs(seed: int = 0) -> dict:
    seeds = jax.random.split(jax.random.key(seed), 8)
    grad_out = centred(seeds[0], (SECTIONS, REPLICAS, TOK_G, D), 1.0, 6.0, ((0, 4), (1, 4), (2, 16)))
    saved_input = centred(seeds[1], (SECTIONS, REPLICAS, TOK_G, D), 1.0, 6.0, ((0, 4), (1, 4), (2, 16)))
    pre_act = centred(seeds[2], (SECTIONS, REPLICAS, TOK_G, HID), 1.5, 8.0, ((0, 4), (1, 4), (3, 16)))
    error = centred(seeds[3], (SECTIONS, REPLICAS, TOK_G, D), 0.4, 3.0, ((0, 4), (1, 4), (2, 16)), jnp.float32)
    w_up = centred(seeds[4], (SECTIONS, D, HID), D ** -0.5, 0.078125, ((0, 4), (1, 4), (2, 16)))
    w_down = centred(seeds[5], (SECTIONS, HID, D), HID ** -0.5, 0.0546875, ((0, 4), (1, 16), (2, 4)))
    q_init = centred(seeds[6], (SECTIONS, D, RANK), D ** -0.5, 0.078125, ((0, 4),))
    return dict(grad_out=grad_out, saved_input=saved_input, pre_act=pre_act, error=error, w_up=w_up, w_down=w_down, q_init=q_init)


def gelu_tanh(values):
    return jax.nn.gelu(values, approximate=True)

def reference(grad_out, saved_input, pre_act, error, w_up, w_down, q_init):
    up_list = []
    down_list = []
    error_list = []
    left_list = []
    right_list = []
    rows = N_DP * TOK_G
    for section_idx in range(N_SECTION):
        grad_rows = grad_out[section_idx].reshape(rows, D)
        input_rows = saved_input[section_idx].reshape(rows, D)
        pre_rows = pre_act[section_idx].reshape(rows, HID).astype(jnp.float32)
        hidden = gelu_tanh(pre_rows).astype(jnp.bfloat16)
        down_list.append(jnp.dot(hidden.T.astype(jnp.float32), grad_rows.astype(jnp.float32), preferred_element_type=jnp.float32).astype(jnp.bfloat16))
        grad_hidden = jnp.dot(grad_rows.astype(jnp.float32), w_down[section_idx].T.astype(jnp.float32), preferred_element_type=jnp.float32)
        grad_pre = jax.vjp(gelu_tanh, pre_rows)[1](grad_hidden)[0].astype(jnp.bfloat16)
        up_list.append(jnp.dot(input_rows.T.astype(jnp.float32), grad_pre.astype(jnp.float32), preferred_element_type=jnp.float32).astype(jnp.bfloat16))
        grad_input = grad_rows.astype(jnp.float32) + jnp.dot(grad_pre.astype(jnp.float32), w_up[section_idx].T.astype(jnp.float32), preferred_element_type=jnp.float32)
        merged_all = grad_input.reshape(N_DP, TOK_G, D) + error[section_idx]
        factor_q = q_init[section_idx].astype(jnp.float32)
        errs = []
        lefts = []
        rights = []
        for replica in range(N_DP):
            merged = merged_all[replica]
            left = jnp.dot(merged, factor_q, precision=lax.Precision.HIGHEST)
            gram = jnp.dot(left.T, left, precision=lax.Precision.HIGHEST)
            lower = jnp.linalg.cholesky(gram)
            ortho = jax.scipy.linalg.solve_triangular(lower, left.T, lower=True).T
            factor_left = ortho.astype(jnp.bfloat16)
            right = jnp.dot(merged.T, factor_left.astype(jnp.float32), precision=lax.Precision.HIGHEST)
            factor_right = right.astype(jnp.bfloat16)
            approx = jnp.dot(factor_left.astype(jnp.float32), factor_right.T.astype(jnp.float32), preferred_element_type=jnp.float32)
            errs.append(merged - approx)
            lefts.append(factor_left)
            rights.append(factor_right)
        error_list.append(jnp.stack(errs))
        left_list.append(lefts)
        right_list.append(rights)
    recv_list = []
    for section_idx in range(N_SECTION):
        if section_idx + 1 < N_SECTION:
            recv_list.append(jnp.stack([jnp.dot(left_list[section_idx + 1][replica].astype(jnp.float32), right_list[section_idx + 1][replica].T.astype(jnp.float32), preferred_element_type=jnp.float32).astype(jnp.bfloat16) for replica in range(N_DP)]))
        else:
            recv_list.append(jnp.zeros((N_DP, TOK_G, D), jnp.bfloat16))
    return (jnp.stack(up_list), jnp.stack(down_list), jnp.stack(error_list), jnp.stack(recv_list))
```

```python
import jax
import jax.numpy as jnp
from jax import lax
from jax.experimental import pallas as pl
from jax.experimental.pallas import tpu as pltpu
from jax.sharding import PartitionSpec as P

BF, F32 = jnp.bfloat16, jnp.float32
MESH = pl.DeviceIdType.MESH
ROWS = 16
GROUP = 256
WIDTH = 1536
HIDDEN = 768
MODEL = 6144
RANK = 128
PIECE = 384
K0 = 0.7978845608
K1 = 0.044715
HIGH = lax.Precision.HIGHEST


class Copies:
    def __init__(self, send, recv):
        self.send, self.recv, self.count, self.made = send, recv, 0, []

    def new(self, src, dst, device):
        at = self.count
        self.count += 1
        copy = pltpu.make_async_remote_copy(
            src_ref=src,
            dst_ref=dst,
            send_sem=self.send.at[at],
            recv_sem=self.recv.at[at],
            device_id=device,
            device_id_type=MESH,
        )
        self.made.append(copy)
        return copy

    def start(self, src, dst, device):
        copy = self.new(src, dst, device)
        copy.start()
        return copy

    def finish(self, skip):
        for copy in self.made:
            if not any(copy is other for other in skip):
                copy.wait_send()


def add_slabs(dst, src, count):
    def body(j, _):
        dst[j] = (dst[j].astype(F32) + src[j].astype(F32)).astype(BF)
        return 0

    lax.fori_loop(0, count, body, 0)


def gelu_value(v):
    return 0.5 * v * (1.0 + jnp.tanh(K0 * (v + K1 * (v * v * v))))


def gelu_slope(v):
    square = v * v
    th = jnp.tanh(K0 * (v + K1 * (square * v)))
    return 0.5 * (1.0 + th) + (0.5 * K0) * v * (1.0 - th * th) * (1.0 + (3.0 * K1) * square)


def block_kernel(
    grad, inp, pre, error, w_down, w_up,
    gdown_out, gup_out, merged_out,
    G, X, PRE, GP, WD, WU, H, HF, RSA, RSB, C, SB, X1, X2, Z, D, BK, GD, GU, OWN, ERR, MRG,
    send, recv, local,
):
    t = lax.axis_index("tensor")
    d = lax.axis_index("dp")
    zl, x, c = t // 8, (t // 2) % 4, t % 2
    xr, xl, xo = (x + 1) % 4, (x + 3) % 4, (x + 2) % 4
    dr, dl, do = (d + 1) % 4, (d + 3) % 4, (d + 2) % 4
    sib = {"tensor": zl * 8 + x * 2 + (1 - c)}
    zpeer = {"tensor": (1 - zl) * 8 + x * 2 + c}
    right = {"tensor": zl * 8 + xr * 2 + c}
    left = {"tensor": zl * 8 + xl * 2 + c}
    dpr, dpl, dpo = {"dp": dr}, {"dp": dl}, {"dp": do}
    net = Copies(send, recv)

    loads = {}

    def load(name, at, src, dst):
        copy = pltpu.make_async_copy(src, dst, local.at[at])
        copy.start()
        loads[name] = copy

    def cols(block):
        return pl.ds(pl.multiple_of(block * WIDTH, 128), WIDTH)

    load("G", 0, grad.at[:, cols(d)], G.at[d, zl, x, c])
    load("X", 1, inp.at[:, cols(d)], X.at[d, zl, x, c])
    load("WD", 2, w_down, WD)
    load("PRE", 3, pre, PRE.at[d])
    load("WU", 4, w_up, WU)
    load("OWN", 5, grad, OWN)
    load("ERR", 6, error, ERR)

    barrier = pltpu.get_barrier_semaphore()
    for device in (sib, zpeer, right, left, dpr, dpl, dpo):
        pl.semaphore_signal(barrier, inc=1, device_id=device, device_id_type=MESH)
    pl.semaphore_wait(barrier, 7)

    def scatter(src, dst):
        return [
            net.start(src.at[:, cols(to)], dst.at[d, zl, x, c], {"dp": to}) for to in (dr, dl, do)
        ]

    order = (do, dr, dl, d)

    def gather_first(buf, r):
        own = buf.at[r, zl, x, c]
        return dict(
            z=net.start(own, own, zpeer),
            r=[net.start(own, own, right)],
            l=[net.start(own, own, left)],
            s=[],
        )

    def gather_second(buf, r, state):
        state["z"].wait_recv()
        other = buf.at[r, 1 - zl, x, c]
        state["r"].append(net.start(other, other, right))
        state["l"].append(net.start(other, other, left))
        pair = buf.at[r, :, x, c]
        state["s"].append(net.start(pair, pair, sib))

    def gather_third(buf, r, state):
        for copy in state["r"]:
            copy.wait_recv()
        part = buf.at[r, 0, xl, c]
        state["fr"] = net.start(part, part, right)
        for copy in state["l"]:
            copy.wait_recv()
        part = buf.at[r, 1, xr, c]
        state["fl"] = net.start(part, part, left)
        for at in (xl, xr):
            pair = buf.at[r, :, at, c]
            state["s"].append(net.start(pair, pair, sib))

    def gather_fourth(buf, r, state):
        state["fr"].wait_recv()
        state["fl"].wait_recv()
        pair = buf.at[r, :, xo, c]
        state["s"].append(net.start(pair, pair, sib))

    def gather_last(state):
        for copy in state["s"]:
            copy.wait_recv()

    first = scatter(grad, G)
    loads["G"].wait()
    for copy in first:
        copy.wait_recv()
    g_states = [gather_first(G, r) for r in order]
    for r, state in zip(order, g_states):
        gather_second(G, r, state)
    x_first = scatter(inp, X)
    pre_r = net.start(pre, PRE.at[d], dpr)
    pre_l = net.start(pre, PRE.at[d], dpl)

    def hidden_part(r, store):
        def body(j, _):
            at = pl.ds(pl.multiple_of(j * 256, 256), 256)
            rows = G[r].reshape(GROUP, WIDTH)
            store(
                at,
                lax.dot_general(
                    rows, WD[at, :], (((1,), (1,)), ((), ())), preferred_element_type=F32
                ),
            )
            return 0

        lax.fori_loop(0, HIDDEN // 256, body, 0)

    def store_bf(k):
        def store(at, value):
            H[k, :, at] = value.astype(BF)

        return store

    def store_own(at, value):
        HF[:, at] = value

    top, low = pl.ds(0, 128), pl.ds(128, 128)
    rsa, rsb = [], {}
    gather_third(G, order[0], g_states[0])
    for k, r in enumerate(order):
        if k + 1 < 4:
            gather_third(G, order[k + 1], g_states[k + 1])
        gather_fourth(G, r, g_states[k])
        if k == 0:
            loads["WD"].wait()
        gather_last(g_states[k])
        hidden_part(r, store_own if k == 3 else store_bf(k))
        if k == 0:
            rsa.append(net.start(H.at[0, top], RSA.at[0], dpr))
            rsa.append(net.start(H.at[0, low], RSA.at[1], dpl))
        if k == 1:
            rsb["r_low"] = net.start(H.at[1, low], RSB.at[0, low], dpr)
        if k == 2:
            rsb["l_top"] = net.start(H.at[2, top], RSB.at[1, top], dpl)

    def add_rows(k, base, part):
        def body(j, _):
            at = pl.ds(pl.multiple_of(base + j * 16, 16), 16)
            at_part = pl.ds(pl.multiple_of(j * 16, 16), 16)
            H[k, at, :] = (H[k, at, :].astype(F32) + RSA[part, at_part, :].astype(F32)).astype(BF)
            return 0

        lax.fori_loop(0, 8, body, 0)

    rsa[0].wait_recv()
    add_rows(1, 0, 0)
    rsb["r_top"] = net.start(H.at[1, top], RSB.at[0, top], dpr)
    rsa[1].wait_recv()
    add_rows(2, 128, 1)
    rsb["l_low"] = net.start(H.at[2, low], RSB.at[1, low], dpl)

    loads["X"].wait()
    for copy in x_first:
        copy.wait_recv()
    x_states = [gather_first(X, r) for r in order]

    def own_slope(base):
        def body(j, _):
            at = pl.ds(pl.multiple_of(base + j * 16, 16), 16)
            total = HF[at, :] + RSB[0, at, :].astype(F32) + RSB[1, at, :].astype(F32)
            GP[d, at, :] = (total * gelu_slope(PRE[d, at, :].astype(F32))).astype(BF)
            return 0

        lax.fori_loop(0, 8, body, 0)

    loads["PRE"].wait()
    gp = {}
    for name, half, base in (("top", top, 0), ("low", low, 128)):
        rsb["r_" + name].wait_recv()
        rsb["l_" + name].wait_recv()
        own_slope(base)
        part = GP.at[d, half]
        gp["r_" + name] = net.start(part, part, dpr)
        gp["l_" + name] = net.start(part, part, dpl)

    def up_part(r):
        def body(j, _):
            at = pl.ds(pl.multiple_of(j * 256, 256), 256)
            value = lax.dot_general(
                GP[r], WU[at, :], (((1,), (1,)), ((), ())), preferred_element_type=F32
            )
            C[r, :, :, :, :, at] = value.astype(BF).reshape(2, 4, 2, 16, 256)
            return 0

        lax.fori_loop(0, WIDTH // 256, body, 0)

    def s1(r, st):
        up_part(r)
        st["s"] = net.start(C.at[r, :, :, 1 - c], SB.at[r], sib)

    def s2(r, st):
        st["s"].wait_recv()

        def body(j, _):
            a, b = j // 4, j % 4
            C[r, a, b, c] = (C[r, a, b, c].astype(F32) + SB[r, a, b].astype(F32)).astype(BF)
            return 0

        lax.fori_loop(0, 8, body, 0)
        st["x1r"] = net.start(C.at[r, 0, xo, c], X1.at[r, 0], right)
        st["x1l"] = net.start(C.at[r, 1, xo, c], X1.at[r, 1], left)

    def s3(r, st):
        st["x1r"].wait_recv()
        C[r, 0, xr, c] = (C[r, 0, xr, c].astype(F32) + X1[r, 0].astype(F32)).astype(BF)
        st["x2r"] = net.start(C.at[r, :, xr, c], X2.at[r, 0], right)
        st["x1l"].wait_recv()
        C[r, 1, xl, c] = (C[r, 1, xl, c].astype(F32) + X1[r, 1].astype(F32)).astype(BF)
        st["x2l"] = net.start(C.at[r, :, xl, c], X2.at[r, 1], left)

    def s4(r, st):
        st["x2r"].wait_recv()
        st["x2l"].wait_recv()
        for a in (0, 1):
            C[r, a, x, c] = (
                C[r, a, x, c].astype(F32) + X2[r, 0, a].astype(F32) + X2[r, 1, a].astype(F32)
            ).astype(BF)
        st["z"] = net.start(C.at[r, 1 - zl, x, c], Z.at[r], zpeer)

    def s5(r, st, own=False):
        st["z"].wait_recv()
        D[r] = (C[r, zl, x, c].astype(F32) + Z[r].astype(F32)).astype(BF)
        if not own:
            st["b"] = net.start(D.at[r], BK.at[d], {"dp": r})

    chain = (d, dl, dr, do)
    st = [dict() for _ in chain]
    loads["WU"].wait()
    s1(chain[0], st[0])
    s2(chain[0], st[0])
    s3(chain[0], st[0])

    gp["r_top"].wait_recv()
    part = GP.at[dl, top]
    gp["fr"] = net.start(part, part, dpr)
    gp["l_low"].wait_recv()
    part = GP.at[dr, low]
    gp["fl"] = net.start(part, part, dpl)
    for r, state in zip(order, x_states):
        gather_second(X, r, state)
    gp["r_low"].wait_recv()
    gp["l_top"].wait_recv()
    s1(chain[1], st[1])
    s1(chain[2], st[2])
    s4(chain[0], st[0])
    s2(chain[1], st[1])
    s2(chain[2], st[2])
    s5(chain[0], st[0], own=True)
    s3(chain[1], st[1])
    s3(chain[2], st[2])
    for r, state in zip(order, x_states):
        gather_third(X, r, state)
    pre_r.wait_recv()
    part = PRE.at[dl, top]
    pre_fr = net.start(part, part, dpr)
    pre_l.wait_recv()
    part = PRE.at[dr, low]
    pre_fl = net.start(part, part, dpl)
    s4(chain[1], st[1])
    s4(chain[2], st[2])
    for r, state in zip(order, x_states):
        gather_fourth(X, r, state)
    s5(chain[1], st[1])
    s5(chain[2], st[2])

    def up_grad(lo, hi):
        def body(j, _):
            at = pl.ds(pl.multiple_of(j * 256, 256), 256)
            rows = X[:, :, :, :, :, at].reshape(4 * GROUP, 256)
            value = lax.dot_general(
                rows,
                GP[...].reshape(4 * GROUP, HIDDEN),
                (((0,), (0,)), ((), ())),
                preferred_element_type=F32,
            )
            GU[at, :] = value.astype(BF)
            return 0

        lax.fori_loop(lo, hi, body, 0)

    def activate():
        def body(j, _):
            at = pl.ds(pl.multiple_of((j % 16) * 16, 16), 16)
            PRE[j // 16, at, :] = gelu_value(PRE[j // 16, at, :].astype(F32)).astype(BF)
            return 0

        lax.fori_loop(0, 64, body, 0)

    def down_grad(lo, hi):
        def body(j, _):
            at = pl.ds(pl.multiple_of(j * 256, 256), 256)
            value = lax.dot_general(
                PRE[:, :, at].reshape(4 * GROUP, 256),
                G[...].reshape(4 * GROUP, WIDTH),
                (((0,), (0,)), ((), ())),
                preferred_element_type=F32,
            )
            GD[at, :] = value.astype(BF)
            return 0

        lax.fori_loop(lo, hi, body, 0)

    gp["fr"].wait_recv()
    gp["fl"].wait_recv()
    s1(chain[3], st[3])
    for state in x_states:
        gather_last(state)
    up_grad(0, 2)
    s2(chain[3], st[3])
    up_grad(2, 4)
    s3(chain[3], st[3])
    up_grad(4, 6)
    load("GU", 7, GU, gup_out)
    s4(chain[3], st[3])
    pre_fr.wait_recv()
    pre_fl.wait_recv()
    pre_fr.wait_send()
    pre_fl.wait_send()
    activate()
    s5(chain[3], st[3])
    down_grad(0, 3)
    load("GD", 8, GD, gdown_out)

    for k in (1, 2, 3):
        st[k]["b"].wait_recv()
    loads["OWN"].wait()
    loads["ERR"].wait()
    BK[d] = D[d]
    for b in range(4):
        at = pl.ds(b * WIDTH, WIDTH)
        MRG[:, at] = OWN[:, at].astype(F32) + ERR[:, at] + BK[b].astype(F32)
    load("MRG", 9, MRG, merged_out)
    for name in ("GU", "GD", "MRG"):
        loads[name].wait()
    net.finish(skip=(pre_fr, pre_fl))


def block_call(grad, inp, pre, error, w_down, w_up):
    vm = pltpu.VMEM
    whole = (4, 2, 4, 2, ROWS, WIDTH)
    any_spec = pl.BlockSpec(memory_space=pl.ANY)
    return pl.pallas_call(
        block_kernel,
        out_shape=(
            jax.ShapeDtypeStruct((HIDDEN, WIDTH), BF),
            jax.ShapeDtypeStruct((WIDTH, HIDDEN), BF),
            jax.ShapeDtypeStruct((ROWS, MODEL), F32),
        ),
        in_specs=[any_spec] * 6,
        out_specs=(any_spec,) * 3,
        scratch_shapes=[
            vm(whole, BF),
            vm(whole, BF),
            vm((4, GROUP, HIDDEN), BF),
            vm((4, GROUP, HIDDEN), BF),
            vm((HIDDEN, WIDTH), BF),
            vm((WIDTH, HIDDEN), BF),
            vm((3, GROUP, HIDDEN), BF),
            vm((GROUP, HIDDEN), F32),
            vm((2, 128, HIDDEN), BF),
            vm((2, GROUP, HIDDEN), BF),
            vm(whole, BF),
            vm((4, 2, 4, ROWS, WIDTH), BF),
            vm((4, 2, ROWS, WIDTH), BF),
            vm((4, 2, 2, ROWS, WIDTH), BF),
            vm((4, ROWS, WIDTH), BF),
            vm((4, ROWS, WIDTH), BF),
            vm((4, ROWS, WIDTH), BF),
            vm((HIDDEN, WIDTH), BF),
            vm((WIDTH, HIDDEN), BF),
            vm((ROWS, MODEL), BF),
            vm((ROWS, MODEL), F32),
            vm((ROWS, MODEL), F32),
            pltpu.SemaphoreType.DMA((160,)),
            pltpu.SemaphoreType.DMA((160,)),
            pltpu.SemaphoreType.DMA((10,)),
        ],
        compiler_params=pltpu.CompilerParams(
            collective_id=0, has_side_effects=True, vmem_limit_bytes=56 * 2**20
        ),
        name="block",
    )(grad, inp, pre, error, w_down, w_up)


def factor_inverse(A):
    rows = lax.broadcasted_iota(jnp.int32, (RANK, 1), 0)
    lanes = lax.broadcasted_iota(jnp.int32, (RANK, RANK), 1)

    def body(k, _):
        pivot = A[pl.ds(k, 1), :]
        gram = A[:, pl.ds(0, RANK)]
        column = jnp.sum(jnp.where(lanes == k, gram, 0.0), axis=1, keepdims=True)
        top = jnp.sum(jnp.where(rows == k, column, 0.0), axis=0, keepdims=True)
        inv = lax.rsqrt(top)
        scaled = pivot * inv
        weight = jnp.where(rows > k, column * inv, 0.0)
        A[...] = jnp.where(rows == k, scaled, A[...] - weight * scaled)
        return 0

    lax.fori_loop(0, RANK, body, 0)


def rank_kernel(
    merged, q, err_out, recv_out,
    MB, STACK, MC, LF, A, AP, AR, RR,
    send, recv, local,
):
    s = lax.axis_index("section")
    t = lax.axis_index("tensor")
    above, below = (s + 1) % 4, (s + 3) % 4

    def peer(k):
        return (t + k) % 16

    barrier = pltpu.get_barrier_semaphore()

    def greet(k, _):
        pl.semaphore_signal(
            barrier, inc=1, device_id={"tensor": peer(k)}, device_id_type=MESH
        )
        return 0

    def greet_other(k, _):
        for other in (above, below):
            pl.semaphore_signal(
                barrier,
                inc=1,
                device_id={"section": other, "tensor": peer(k)},
                device_id_type=MESH,
            )
        return 0

    lax.fori_loop(1, 16, greet, 0)
    lax.fori_loop(0, 16, greet_other, 0)
    pl.semaphore_wait(barrier, 47)

    def rc(src, dst, at, device):
        return pltpu.make_async_remote_copy(
            src_ref=src,
            dst_ref=dst,
            send_sem=send.at[at],
            recv_sem=recv.at[at],
            device_id=device,
            device_id_type=MESH,
        )

    def loop(lo, fn):
        def body(k, _):
            fn(k)
            return 0

        lax.fori_loop(lo, 16, body, 0)

    high = merged[...].astype(BF)
    STACK[pl.ds(0, 16), :] = high
    STACK[pl.ds(16, 16), :] = (merged[...] - high.astype(F32)).astype(BF)
    for b in range(16):
        MB[b] = STACK[pl.ds(0, 16), pl.ds(b * PIECE, PIECE)]
    both = jnp.dot(STACK[...], q[...], preferred_element_type=F32)
    LF[t] = both[:16] + both[16:]

    def left_copy(k):
        return rc(LF.at[t], LF.at[t], k, {"tensor": peer(k)})

    def block_copy(k):
        return rc(MB.at[peer(k)], MC.at[t], 16 + k, {"tensor": peer(k)})

    loop(1, lambda k: left_copy(k).start())
    loop(1, lambda k: block_copy(k).start())
    MC[t] = MB[t]
    loop(1, lambda k: left_copy(k).wait_recv())
    all_left = LF[...].reshape(GROUP, RANK)
    A[:, pl.ds(0, RANK)] = lax.dot_general(
        all_left, all_left, (((0,), (0,)), ((), ())), precision=HIGH, preferred_element_type=F32
    )
    A[:, pl.ds(RANK, RANK)] = (
        lax.broadcasted_iota(jnp.int32, (RANK, RANK), 0)
        == lax.broadcasted_iota(jnp.int32, (RANK, RANK), 1)
    ).astype(F32)
    factor_inverse(A)
    ortho = lax.dot_general(
        all_left, A[:, pl.ds(RANK, RANK)], (((1,), (1,)), ((), ())),
        precision=HIGH, preferred_element_type=F32,
    ).astype(BF)
    loop(1, lambda k: block_copy(k).wait_recv())
    right = lax.dot_general(
        MC[...].reshape(GROUP, PIECE), ortho, (((0,), (0,)), ((), ())), preferred_element_type=F32
    ).astype(BF)
    approx = lax.dot_general(
        ortho, right, (((1,), (1,)), ((), ())), preferred_element_type=F32
    ).astype(BF)
    AP[...] = approx.reshape(16, ROWS, PIECE)

    def back_copy(k):
        return rc(AP.at[peer(k)], AR.at[t], 32 + k, {"tensor": peer(k)})

    def relay_copy(k):
        return rc(AP.at[peer(k)], RR.at[t], 48 + k, {"section": below, "tensor": peer(k)})

    loop(1, lambda k: back_copy(k).start())
    loop(0, lambda k: relay_copy(k).start())
    AR[t] = AP[t]
    loop(1, lambda k: back_copy(k).wait_recv())
    for b in range(16):
        at = pl.ds(b * PIECE, PIECE)
        err_out[:, at] = merged[:, at] - AR[b].astype(F32)
    loop(0, lambda k: relay_copy(k).wait_recv())
    for b in range(16):
        at = pl.ds(b * PIECE, PIECE)
        recv_out[:, at] = jnp.where(s == 3, jnp.zeros((ROWS, PIECE), BF), RR[b])
    loop(1, lambda k: left_copy(k).wait_send())
    loop(1, lambda k: block_copy(k).wait_send())
    loop(1, lambda k: back_copy(k).wait_send())
    loop(0, lambda k: relay_copy(k).wait_send())


def rank_call(merged, q):
    vm = pltpu.VMEM
    vm_spec = pl.BlockSpec(memory_space=pltpu.VMEM)
    return pl.pallas_call(
        rank_kernel,
        out_shape=(
            jax.ShapeDtypeStruct((ROWS, MODEL), F32),
            jax.ShapeDtypeStruct((ROWS, MODEL), BF),
        ),
        in_specs=[vm_spec] * 2,
        out_specs=(vm_spec,) * 2,
        scratch_shapes=[
            vm((16, ROWS, PIECE), BF),
            vm((2 * ROWS, MODEL), BF),
            vm((16, ROWS, PIECE), BF),
            vm((16, ROWS, RANK), F32),
            vm((RANK, 2 * RANK), F32),
            vm((16, ROWS, PIECE), BF),
            vm((16, ROWS, PIECE), BF),
            vm((16, ROWS, PIECE), BF),
            pltpu.SemaphoreType.DMA((64,)),
            pltpu.SemaphoreType.DMA((64,)),
            pltpu.SemaphoreType.DMA((2,)),
        ],
        compiler_params=pltpu.CompilerParams(
            collective_id=1, has_side_effects=True, vmem_limit_bytes=32 * 2**20
        ),
        name="rank",
    )(merged, q)


def shards(grad_out, saved_input, pre_act, error, w_up, w_down, q_init):
    grad_down, grad_up, merged = block_call(
        grad_out[0, 0], saved_input[0, 0], pre_act[0, 0], error[0, 0], w_down[0], w_up[0]
    )
    new_error, received = rank_call(merged, q_init[0])
    return (grad_up[None], grad_down[None], new_error[None, None], received[None, None])


def solution(mesh):
    in_specs = (
        P("section", "dp", "tensor", None),
        P("section", "dp", "tensor", None),
        P("section", "dp", None, "tensor"),
        P("section", "dp", "tensor", None),
        P("section", "dp", "tensor"),
        P("section", "tensor", "dp"),
        P("section", None, None),
    )
    out_specs = (
        P("section", "dp", "tensor"),
        P("section", "tensor", "dp"),
        P("section", "dp", "tensor", None),
        P("section", "dp", "tensor", None),
    )
    return jax.shard_map(shards, mesh=mesh, in_specs=in_specs, out_specs=out_specs, check_vma=False)
```

```python
import jax
import jax.numpy as jnp
from jax import lax
from jax.experimental import pallas as pl
from jax.experimental.pallas import tpu as pltpu
from jax.sharding import PartitionSpec as P

BF, F32 = jnp.bfloat16, jnp.float32
MESH = pl.DeviceIdType.MESH
ROWS = 16
GROUP = 256
WIDTH = 1536
HIDDEN = 768
MODEL = 6144
RANK = 128
PIECE = 384
PARTS = (4, 4, 1, 1)
K0 = 0.7978845608
K1 = 0.044715
HIGH = lax.Precision.HIGHEST


class Tracked:
    def __init__(self, copy):
        self.copy, self.sent, self.received = copy, False, False

    def start(self):
        self.copy.start()

    def wait_send(self):
        self.copy.wait_send()
        self.sent = True

    def wait_recv(self):
        self.copy.wait_recv()
        self.received = True


class Copies:
    def __init__(self, send, recv):
        self.send, self.recv, self.count, self.made = send, recv, 0, []

    def new(self, src, dst, device):
        at = self.count
        self.count += 1
        copy = pltpu.make_async_remote_copy(
            src_ref=src,
            dst_ref=dst,
            send_sem=self.send.at[at],
            recv_sem=self.recv.at[at],
            device_id=device,
            device_id_type=MESH,
        )
        copy = Tracked(copy)
        self.made.append(copy)
        return copy

    def start(self, src, dst, device):
        copy = self.new(src, dst, device)
        copy.start()
        return copy

    def finish(self):
        for copy in self.made:
            if not copy.sent:
                copy.wait_send()


def add_slabs(dst, src, count):
    def body(j, _):
        dst[j] = (dst[j].astype(F32) + src[j].astype(F32)).astype(BF)
        return 0

    lax.fori_loop(0, count, body, 0)


def gelu_value(v):
    return 0.5 * v * (1.0 + jnp.tanh(K0 * (v + K1 * (v * v * v))))


def gelu_slope(v):
    square = v * v
    th = jnp.tanh(K0 * (v + K1 * (square * v)))
    return 0.5 * (1.0 + th) + (0.5 * K0) * v * (1.0 - th * th) * (1.0 + (3.0 * K1) * square)


def factor_inverse(A):
    rows = lax.broadcasted_iota(jnp.int32, (16, RANK), 0)
    lanes = lax.broadcasted_iota(jnp.int32, (16, RANK), 1)
    rows2 = lax.broadcasted_iota(jnp.int32, (16, 2 * RANK), 0)

    def wide(value):
        return jnp.concatenate([value, value], axis=1)

    def body(p, _):
        base = pl.multiple_of(p * 16, 16)
        panel = A[pl.ds(base, 16), :]
        gram = panel[:, :RANK]
        cols = [
            jnp.broadcast_to(
                jnp.sum(jnp.where(lanes == base + j, gram, 0.0), axis=1, keepdims=True), (16, RANK)
            )
            for j in range(16)
        ]
        out = jnp.zeros((16, 2 * RANK), F32)
        for k in range(0, 16, 2):
            one, two = cols[k], cols[k + 1]
            a, b, e = one[k : k + 1], two[k : k + 1], two[k + 1 : k + 2]
            det = a * e - b * b
            inv = 1.0 / det
            below = rows >= k + 2
            m0 = jnp.where(below, (e * one - b * two) * inv, 0.0)
            m1 = jnp.where(below, (a * two - b * one) * inv, 0.0)
            for j in range(k + 2, 16):
                cols[j] = cols[j] - (m0 * cols[j][k : k + 1] + m1 * cols[j][k + 1 : k + 2])
            row0, row1 = panel[k : k + 1], panel[k + 1 : k + 2]
            panel = panel - (wide(m0) * row0 + wide(m1) * row1)
            inv_a = 1.0 / a
            scale0 = lax.rsqrt(a)
            scale1 = lax.rsqrt(det * inv_a)
            new0 = row0 * wide(scale0)
            new1 = (row1 - wide(b * inv_a) * row0) * wide(scale1)
            out = jnp.where(rows2 == k, new0, jnp.where(rows2 == k + 1, new1, out))
        A[pl.ds(base, 16), :] = out
        weights = jnp.where(lanes >= base + 16, out[:, :RANK], 0.0)
        A[...] = A[...] - lax.dot_general(
            weights, out, (((0,), (0,)), ((), ())), precision=HIGH, preferred_element_type=F32
        )
        return 0

    lax.fori_loop(0, RANK // 16, body, 0)


def kernel(
    grad, inp, pre, error, w_down, w_up, q_init,
    gdown_out, gup_out, err_out, recv_out,
    G, X, PRE, GP, WD, WU, H, HF, RSA, RSB, C, SB, X2, BK, GD, GU, OWN, ERR, MRG,
    Q, MB, STACK, MC, LF, A, AP, AR, RR,
    send, recv, send_rank, recv_rank, local,
):
    s = lax.axis_index("section")
    t = lax.axis_index("tensor")
    d = lax.axis_index("dp")
    zl, x, c = t // 8, (t // 2) % 4, t % 2
    xr, xl, xo = (x + 1) % 4, (x + 3) % 4, (x + 2) % 4
    dr, dl, do = (d + 1) % 4, (d + 3) % 4, (d + 2) % 4
    above, below = (s + 1) % 4, (s + 3) % 4
    other_z = (1 - zl) * 8 + x * 2 + c
    sib = {"tensor": zl * 8 + x * 2 + (1 - c)}
    zpeer = {"tensor": other_z}
    right = {"tensor": zl * 8 + xr * 2 + c}
    left = {"tensor": zl * 8 + xl * 2 + c}
    opposite = {"tensor": zl * 8 + xo * 2 + c}
    dpr, dpl = {"dp": dr}, {"dp": dl}
    net = Copies(send, recv)

    def peer(k):
        return (t + k) % 16

    def loop(lo, fn):
        def body(k, _):
            fn(k)
            return 0

        lax.fori_loop(lo, 16, body, 0)

    loads = {}

    def done(name):
        loads[name].wait()


    def load(name, src, dst):
        copy = pltpu.make_async_copy(src, dst, local.at[len(loads)])
        copy.start()
        loads[name] = copy

    def cols(block):
        return pl.ds(pl.multiple_of(block * WIDTH, 128), WIDTH)

    def hail(device):
        pl.semaphore_signal(barrier, inc=1, device_id=device, device_id_type=MESH)

    barrier = pltpu.get_barrier_semaphore()
    for to in (do, dr, dl):
        hail({"dp": to})
        hail({"tensor": other_z, "dp": to})
    loop(1, lambda k: hail({"tensor": peer(k)}))
    loop(0, lambda k: hail({"section": above, "tensor": peer(k)}))
    loop(0, lambda k: hail({"section": below, "tensor": peer(k)}))
    load("G", grad.at[:, cols(d)], G.at[d, zl, x, c])
    load("X", inp.at[:, cols(d)], X.at[d, zl, x, c])
    load("WD", w_down, WD)
    load("PRE", pre, PRE.at[d])
    load("WU", w_up, WU)
    load("OWN", grad, OWN)
    load("ERR", error, ERR)
    load("Q", q_init, Q)
    pl.semaphore_wait(barrier, 53)


    targets = (do, dr, dl, d)

    def scatter(src, dst, k):
        to = targets[k]
        part = dst.at[d, zl, x, c]
        made = [net.start(src.at[:, cols(to)], part, {"tensor": other_z, "dp": to})]
        if k < 3:
            made.append(net.start(src.at[:, cols(to)], part, {"dp": to}))
        return made

    order = (do, dr, dl, d)
    arrive = (0, 2, 1, 3)

    def gather_first(buf, r, copies):
        for copy in copies:
            copy.wait_recv()
        pair = buf.at[r, :, x, c]
        return dict(
            x=[net.start(pair, pair, device) for device in (right, left, opposite)],
            s=[net.start(pair, pair, sib)],
        )

    def gather_second(buf, r, state):
        for copy, at in zip(state["x"], (xl, xr, xo)):
            copy.wait_recv()
            pair = buf.at[r, :, at, c]
            state["s"].append(net.start(pair, pair, sib))

    def gather_last(state):
        for copy in state["s"]:
            copy.wait_recv()

    g_scatter = [scatter(grad, G, 0)]
    done("G")
    g_states = [gather_first(G, order[0], g_scatter[0])]
    g_scatter += [scatter(grad, G, k) for k in (1, 2, 3)]
    for copies in g_scatter:
        for copy in copies:
            copy.wait_send()
    x_scatter = [scatter(inp, X, k) for k in range(4)]

    def hidden_part(r, store):
        store(
            lax.dot_general(
                G[r].reshape(GROUP, WIDTH),
                WD[...],
                (((1,), (1,)), ((), ())),
                preferred_element_type=F32,
            )
        )

    def store_bf(k):
        def store(value):
            H[k] = value.astype(BF)

        return store

    def store_own(value):
        HF[...] = value

    top = [pl.ds(0, 64), pl.ds(64, 64)]
    low = [pl.ds(128, 64), pl.ds(192, 64)]
    rsa, early, late = [], [], []
    for k, r in enumerate(order):
        gather_second(G, r, g_states[k])
        if k == 0:
            for n in (1, 2):
                g_states.append(gather_first(G, order[n], g_scatter[arrive[n]]))
            done("WD")
        if k == 2:
            g_states.append(gather_first(G, order[3], g_scatter[arrive[3]]))
        gather_last(g_states[k])
        hidden_part(r, store_own if k == 3 else store_bf(k))
        if k == 0:
            for q in (0, 1):
                rsa.append(
                    (
                        net.start(H.at[0, top[q]], RSA.at[0, top[q]], dpr),
                        net.start(H.at[0, low[q]], RSA.at[1, top[q]], dpl),
                    )
                )
        if k == 1:
            early_r = net.start(H.at[1, low[0]], RSB.at[0, low[0]], dpr)
        if k == 2:
            early.append((early_r, net.start(H.at[2, top[0]], RSB.at[1, top[0]], dpl)))


    def add_rows(k, base, part, q):
        def body(j, _):
            at = pl.ds(pl.multiple_of(base + q * 64 + j * 16, 16), 16)
            at_part = pl.ds(pl.multiple_of(q * 64 + j * 16, 16), 16)
            H[k, at, :] = (H[k, at, :].astype(F32) + RSA[part, at_part, :].astype(F32)).astype(BF)
            return 0

        lax.fori_loop(0, 4, body, 0)

    done("X")
    x_states = [gather_first(X, order[k], x_scatter[arrive[k]]) for k in range(4)]

    for q in (0, 1):
        rsa[q][0].wait_recv()
        add_rows(1, 0, 0, q)
        late_r = net.start(H.at[1, top[q]], RSB.at[0, top[q]], dpr)
        rsa[q][1].wait_recv()
        add_rows(2, 128, 1, q)
        late.append((late_r, net.start(H.at[2, low[q]], RSB.at[1, low[q]], dpl)))
        if q == 0:
            early.append(
                (
                    net.start(H.at[1, low[1]], RSB.at[0, low[1]], dpr),
                    net.start(H.at[2, top[1]], RSB.at[1, top[1]], dpl),
                )
            )

    def own_slope(half, q):
        def body(j, _):
            at = pl.ds(pl.multiple_of(half * 128 + q * 64 + j * 16, 16), 16)
            to = pl.ds(pl.multiple_of(q * 64 + j * 16, 16), 16)
            total = HF[at, :] + RSB[0, at, :].astype(F32) + RSB[1, at, :].astype(F32)
            GP[d, half, to, :] = (total * gelu_slope(PRE[d, at, :].astype(F32))).astype(BF)
            return 0

        lax.fori_loop(0, 4, body, 0)

    done("PRE")
    gp = []
    for q in (0, 1):
        for copy in early[q] + late[q]:
            copy.wait_recv()
        own_slope(0, q)
        own_slope(1, q)
        part = GP.at[d, :, top[q]]
        gp.append((net.start(part, part, dpr), net.start(part, part, dpl)))

    def pass_on(q):
        gp[q][0].wait_recv()
        part = GP.at[dl, 0, top[q]]
        one = net.start(part, part, dpr)
        gp[q][1].wait_recv()
        part = GP.at[dr, 1, top[q]]
        return one, net.start(part, part, dpl)

    def up_part(r):
        def body(j, _):
            at = pl.ds(pl.multiple_of(j * 768, 256), 768)
            value = lax.dot_general(
                GP[r].reshape(GROUP, HIDDEN),
                WU[at, :],
                (((1,), (1,)), ((), ())),
                preferred_element_type=F32,
            )
            C[r, :, :, :, :, at] = value.astype(BF).reshape(2, 4, 2, 16, 768)
            return 0

        lax.fori_loop(0, WIDTH // 768, body, 0)

    def s1(r, st):
        up_part(r)
        st["s"] = net.start(C.at[r, :, :, 1 - c], SB.at[r], sib)

    def s2(r, st):
        st["s"].wait_recv()

        def add(at):
            def body(a, _):
                C[r, a, at, c] = (
                    C[r, a, at, c].astype(F32) + SB[r, a, at].astype(F32)
                ).astype(BF)
                return 0

            lax.fori_loop(0, 2, body, 0)

        st["x"] = []
        for at, slot, device in ((xo, 2, opposite), (xr, 0, right), (xl, 1, left)):
            add(at)
            st["x"].append(net.start(C.at[r, :, at, c], X2.at[r, slot], device))
        add(x)

    def s4(r, st, own=False):
        for copy in st["x"]:
            copy.wait_recv()
        for a in (0, 1):
            C[r, a, x, c] = (
                (C[r, a, x, c].astype(F32) + X2[r, 0, a].astype(F32))
                + (X2[r, 1, a].astype(F32) + X2[r, 2, a].astype(F32))
            ).astype(BF)
        same, across = C.at[r, zl, x, c], C.at[r, 1 - zl, x, c]
        if own:
            st["b"] = [net.start(across, BK.at[d, zl], zpeer)]
            BK[d, zl] = C[d, zl, x, c]
        else:
            st["b"] = [
                net.start(same, BK.at[d, zl], {"dp": r}),
                net.start(across, BK.at[d, zl], {"tensor": other_z, "dp": r}),
            ]

    chain = (d, dl, dr, do)
    st = [dict() for _ in chain]
    for r, state in zip(order, x_states):
        gather_second(X, r, state)
    done("WU")
    s1(chain[0], st[0])
    fwd = [pass_on(0)]
    s2(chain[0], st[0])
    fwd.append(pass_on(1))
    s1(chain[1], st[1])
    s1(chain[2], st[2])
    s4(chain[0], st[0], own=True)
    s2(chain[1], st[1])
    s2(chain[2], st[2])

    def up_grad(lo, hi):
        def body(j, _):
            at = pl.ds(pl.multiple_of(j * 256, 256), 256)
            rows = X[:, :, :, :, :, at].reshape(4 * GROUP, 256)
            value = lax.dot_general(
                rows,
                GP[...].reshape(4 * GROUP, HIDDEN),
                (((0,), (0,)), ((), ())),
                preferred_element_type=F32,
            )
            GU[at, :] = value.astype(BF)
            return 0

        lax.fori_loop(lo, hi, body, 0)

    def activate(r):
        def body(j, _):
            at = pl.ds(pl.multiple_of(j * 16, 16), 16)
            PRE[r, at, :] = gelu_value(PRE[r, at, :].astype(F32)).astype(BF)
            return 0

        lax.fori_loop(0, 16, body, 0)

    def down_grad(lo, hi):
        def body(j, _):
            at = pl.ds(pl.multiple_of(j * 256, 256), 256)
            value = lax.dot_general(
                PRE[:, :, at].reshape(4 * GROUP, 256),
                G[...].reshape(4 * GROUP, WIDTH),
                (((0,), (0,)), ((), ())),
                preferred_element_type=F32,
            )
            GD[at, :] = value.astype(BF)
            return 0

        lax.fori_loop(lo, hi, body, 0)

    for pair in fwd:
        for copy in pair:
            copy.wait_recv()
    pre_part = [pre.at[pl.ds(0, 128)], pre.at[pl.ds(128, 128)]]
    pre_to = [PRE.at[d, pl.ds(0, 128)], PRE.at[d, pl.ds(128, 128)]]
    pre_a = (net.start(pre_part[0], pre_to[0], dpr), net.start(pre_part[1], pre_to[1], dpl))
    s1(chain[3], st[3])
    s4(chain[1], st[1])
    s4(chain[2], st[2])
    for state in x_states:
        gather_last(state)
    s2(chain[3], st[3])
    pre_b = (net.start(pre_part[1], pre_to[1], dpr), net.start(pre_part[0], pre_to[0], dpl))
    up_grad(0, 6)
    load("GU", GU, gup_out)
    s4(chain[3], st[3])
    pre_a[0].wait_recv()
    part = PRE.at[dl, pl.ds(0, 128)]
    pre_fr = net.start(part, part, dpr)
    pre_a[1].wait_recv()
    part = PRE.at[dr, pl.ds(128, 128)]
    pre_fl = net.start(part, part, dpl)
    activate(d)

    done("OWN")
    done("ERR")
    for k in range(4):
        for copy in st[k]["b"]:
            copy.wait_recv()
    for b in range(4):
        at = pl.ds(b * WIDTH, WIDTH)
        block = BK[b, 0].astype(F32) + BK[b, 1].astype(F32)
        merged = OWN[:, at].astype(F32) + ERR[:, at] + block
        MRG[:, at] = merged
        high = merged.astype(BF)
        STACK[pl.ds(0, 16), at] = high
        STACK[pl.ds(16, 16), at] = (merged - high.astype(F32)).astype(BF)
    done("Q")
    both = jnp.dot(STACK[...], Q[...], preferred_element_type=F32)
    LF[t] = both[:16] + both[16:]

    def rc(src, dst, at, device):
        return pltpu.make_async_remote_copy(
            src_ref=src,
            dst_ref=dst,
            send_sem=send_rank.at[at],
            recv_sem=recv_rank.at[at],
            device_id=device,
            device_id_type=MESH,
        )

    def left_copy(k):
        return rc(LF.at[t], LF.at[t], k, {"tensor": peer(k)})

    def block_copy(k):
        return rc(MB.at[peer(k)], MC.at[t], 16 + k, {"tensor": peer(k)})

    def back_copy(k):
        return rc(AP.at[peer(k)], AR.at[t], 32 + k, {"tensor": peer(k)})

    def relay_copy(k):
        return rc(AP.at[peer(k)], RR.at[t], 48 + k, {"section": below, "tensor": peer(k)})

    loop(1, lambda k: left_copy(k).start())
    for b in range(16):
        MB[b] = STACK[pl.ds(0, 16), pl.ds(b * PIECE, PIECE)]
    loop(1, lambda k: block_copy(k).start())
    MC[t] = MB[t]
    A[:, pl.ds(RANK, RANK)] = (
        lax.broadcasted_iota(jnp.int32, (RANK, RANK), 0)
        == lax.broadcasted_iota(jnp.int32, (RANK, RANK), 1)
    ).astype(F32)
    loop(1, lambda k: left_copy(k).wait_recv())
    all_left = LF[...].reshape(GROUP, RANK)
    A[:, pl.ds(0, RANK)] = lax.dot_general(
        all_left, all_left, (((0,), (0,)), ((), ())), precision=HIGH, preferred_element_type=F32
    )
    factor_inverse(A)
    ortho = lax.dot_general(
        all_left, A[:, pl.ds(RANK, RANK)], (((1,), (1,)), ((), ())),
        precision=HIGH, preferred_element_type=F32,
    ).astype(BF)
    loop(1, lambda k: block_copy(k).wait_recv())
    factor = lax.dot_general(
        MC[...].reshape(GROUP, PIECE), ortho, (((0,), (0,)), ((), ())), preferred_element_type=F32
    ).astype(BF)
    approx = lax.dot_general(
        ortho, factor, (((1,), (1,)), ((), ())), preferred_element_type=F32
    ).astype(BF)
    AP[...] = approx.reshape(16, ROWS, PIECE)
    loop(1, lambda k: back_copy(k).start())
    loop(0, lambda k: relay_copy(k).start())
    AR[t] = AP[t]

    for copy in pre_b + (pre_fr, pre_fl):
        copy.wait_recv()
    pre_fr.wait_send()
    pre_fl.wait_send()
    for r in (dl, dr, do):
        activate(r)
    down_grad(0, 3)
    load("GD", GD, gdown_out)
    loop(1, lambda k: back_copy(k).wait_recv())
    for b in range(16):
        at = pl.ds(b * PIECE, PIECE)
        err_out[:, at] = MRG[:, at] - AR[b].astype(F32)
    loop(0, lambda k: relay_copy(k).wait_recv())
    for b in range(16):
        at = pl.ds(b * PIECE, PIECE)
        recv_out[:, at] = jnp.where(s == 3, jnp.zeros((ROWS, PIECE), BF), RR[b])
    loop(1, lambda k: left_copy(k).wait_send())
    loop(1, lambda k: block_copy(k).wait_send())
    loop(1, lambda k: back_copy(k).wait_send())
    loop(0, lambda k: relay_copy(k).wait_send())
    done("GU")
    done("GD")
    net.finish()


def call(grad, inp, pre, error, w_down, w_up, q):
    vm = pltpu.VMEM
    whole = (4, 2, 4, 2, ROWS, WIDTH)
    any_spec = pl.BlockSpec(memory_space=pl.ANY)
    vm_spec = pl.BlockSpec(memory_space=pltpu.VMEM)
    return pl.pallas_call(
        kernel,
        out_shape=(
            jax.ShapeDtypeStruct((HIDDEN, WIDTH), BF),
            jax.ShapeDtypeStruct((WIDTH, HIDDEN), BF),
            jax.ShapeDtypeStruct((ROWS, MODEL), F32),
            jax.ShapeDtypeStruct((ROWS, MODEL), BF),
        ),
        in_specs=[any_spec] * 7,
        out_specs=(any_spec, any_spec, vm_spec, vm_spec),
        scratch_shapes=[
            vm(whole, BF),
            vm(whole, BF),
            vm((4, GROUP, HIDDEN), BF),
            vm((4, 2, 128, HIDDEN), BF),
            vm((HIDDEN, WIDTH), BF),
            vm((WIDTH, HIDDEN), BF),
            vm((3, GROUP, HIDDEN), BF),
            vm((GROUP, HIDDEN), F32),
            vm((2, 128, HIDDEN), BF),
            vm((2, GROUP, HIDDEN), BF),
            vm(whole, BF),
            vm((4, 2, 4, ROWS, WIDTH), BF),
            vm((4, 3, 2, ROWS, WIDTH), BF),
            vm((4, 2, ROWS, WIDTH), BF),
            vm((HIDDEN, WIDTH), BF),
            vm((WIDTH, HIDDEN), BF),
            vm((ROWS, MODEL), BF),
            vm((ROWS, MODEL), F32),
            vm((ROWS, MODEL), F32),
            vm((MODEL, RANK), BF),
            vm((16, ROWS, PIECE), BF),
            vm((2 * ROWS, MODEL), BF),
            vm((16, ROWS, PIECE), BF),
            vm((16, ROWS, RANK), F32),
            vm((RANK, 2 * RANK), F32),
            vm((16, ROWS, PIECE), BF),
            vm((16, ROWS, PIECE), BF),
            vm((16, ROWS, PIECE), BF),
            pltpu.SemaphoreType.DMA((140,)),
            pltpu.SemaphoreType.DMA((140,)),
            pltpu.SemaphoreType.DMA((64,)),
            pltpu.SemaphoreType.DMA((64,)),
            pltpu.SemaphoreType.DMA((10,)),
        ],
        compiler_params=pltpu.CompilerParams(
            collective_id=0, has_side_effects=True, vmem_limit_bytes=58 * 2**20
        ),
        name="block",
    )(grad, inp, pre, error, w_down, w_up, q)


def copy_kernel(*refs):
    sem = refs[12]
    pieces = []
    for n in range(4):
        src, dst, held = refs[n], refs[4 + n], refs[8 + n]
        step = src.shape[0] // PARTS[n]
        for k in range(PARTS[n]):
            at = pl.ds(k * step, step)
            to = len(pieces)
            load = pltpu.make_async_copy(src.at[at], held.at[at], sem.at[0, to])
            load.start()
            store = pltpu.make_async_copy(held.at[at], dst.at[at], sem.at[1, to])
            pieces.append((load, store))
    for load, store in pieces:
        load.wait()
        store.start()
    for load, store in pieces:
        store.wait()


def copy_call(values):
    any_spec = pl.BlockSpec(memory_space=pl.ANY)
    return pl.pallas_call(
        copy_kernel,
        out_shape=tuple(jax.ShapeDtypeStruct(v.shape, v.dtype) for v in values),
        in_specs=[any_spec] * 4,
        out_specs=(any_spec,) * 4,
        scratch_shapes=[pltpu.VMEM(v.shape, v.dtype) for v in values]
        + [pltpu.SemaphoreType.DMA((2, sum(PARTS)))],
        compiler_params=pltpu.CompilerParams(vmem_limit_bytes=16 * 2**20),
        name="deliver",
    )(*values)


def shards(grad_out, saved_input, pre_act, error, w_up, w_down, q_init):
    grad_down, grad_up, new_error, received = call(
        grad_out[0, 0], saved_input[0, 0], pre_act[0, 0], error[0, 0], w_down[0], w_up[0], q_init[0]
    )
    grad_down, grad_up, new_error, received = copy_call((grad_down, grad_up, new_error, received))
    return (grad_up[None], grad_down[None], new_error[None, None], received[None, None])


def solution(mesh):
    in_specs = (
        P("section", "dp", "tensor", None),
        P("section", "dp", "tensor", None),
        P("section", "dp", None, "tensor"),
        P("section", "dp", "tensor", None),
        P("section", "dp", "tensor"),
        P("section", "tensor", "dp"),
        P("section", None, None),
    )
    out_specs = (
        P("section", "dp", "tensor"),
        P("section", "tensor", "dp"),
        P("section", "dp", "tensor", None),
        P("section", "dp", "tensor", None),
    )
    return jax.shard_map(shards, mesh=mesh, in_specs=in_specs, out_specs=out_specs, check_vma=False)
```

```python
import jax
import jax.numpy as jnp
from jax import lax
from jax.experimental import pallas as pl
from jax.experimental.pallas import tpu as pltpu
from jax.sharding import PartitionSpec as P

BF, F32 = jnp.bfloat16, jnp.float32
MESH = pl.DeviceIdType.MESH
ROWS = 16
GROUP = 256
WIDTH = 1536
HIDDEN = 768
MODEL = 6144
RANK = 128
PIECE = 384
PARTS = (4, 4, 1, 1)
K0 = 0.7978845608
K1 = 0.044715
HIGH = lax.Precision.HIGHEST


class Tracked:
    def __init__(self, copy):
        self.copy, self.sent, self.received = copy, False, False

    def start(self):
        self.copy.start()

    def wait_send(self):
        self.copy.wait_send()
        self.sent = True

    def wait_recv(self):
        self.copy.wait_recv()
        self.received = True


class Copies:
    def __init__(self, send, recv):
        self.send, self.recv, self.count, self.made = send, recv, 0, []

    def new(self, src, dst, device):
        at = self.count
        self.count += 1
        copy = pltpu.make_async_remote_copy(
            src_ref=src,
            dst_ref=dst,
            send_sem=self.send.at[at],
            recv_sem=self.recv.at[at],
            device_id=device,
            device_id_type=MESH,
        )
        copy = Tracked(copy)
        self.made.append(copy)
        return copy

    def start(self, src, dst, device):
        copy = self.new(src, dst, device)
        copy.start()
        return copy

    def finish(self):
        for copy in self.made:
            if not copy.sent:
                copy.wait_send()


def add_slabs(dst, src, count):
    def body(j, _):
        dst[j] = (dst[j].astype(F32) + src[j].astype(F32)).astype(BF)
        return 0

    lax.fori_loop(0, count, body, 0)


def gelu_value(v):
    return 0.5 * v * (1.0 + jnp.tanh(K0 * (v + K1 * (v * v * v))))


def gelu_slope(v):
    square = v * v
    th = jnp.tanh(K0 * (v + K1 * (square * v)))
    return 0.5 * (1.0 + th) + (0.5 * K0) * v * (1.0 - th * th) * (1.0 + (3.0 * K1) * square)


def factor_inverse(A):
    rows = lax.broadcasted_iota(jnp.int32, (16, RANK), 0)
    lanes = lax.broadcasted_iota(jnp.int32, (16, RANK), 1)
    rows2 = lax.broadcasted_iota(jnp.int32, (16, 2 * RANK), 0)

    def wide(value):
        return jnp.concatenate([value, value], axis=1)

    def body(p, _):
        base = pl.multiple_of(p * 16, 16)
        panel = A[pl.ds(base, 16), :]
        gram = panel[:, :RANK]
        cols = [
            jnp.broadcast_to(
                jnp.sum(jnp.where(lanes == base + j, gram, 0.0), axis=1, keepdims=True), (16, RANK)
            )
            for j in range(16)
        ]
        out = jnp.zeros((16, 2 * RANK), F32)
        for k in range(0, 16, 2):
            one, two = cols[k], cols[k + 1]
            a, b, e = one[k : k + 1], two[k : k + 1], two[k + 1 : k + 2]
            det = a * e - b * b
            inv = 1.0 / det
            below = rows >= k + 2
            m0 = jnp.where(below, (e * one - b * two) * inv, 0.0)
            m1 = jnp.where(below, (a * two - b * one) * inv, 0.0)
            for j in range(k + 2, 16):
                cols[j] = cols[j] - (m0 * cols[j][k : k + 1] + m1 * cols[j][k + 1 : k + 2])
            row0, row1 = panel[k : k + 1], panel[k + 1 : k + 2]
            panel = panel - (wide(m0) * row0 + wide(m1) * row1)
            inv_a = 1.0 / a
            scale0 = lax.rsqrt(a)
            scale1 = lax.rsqrt(det * inv_a)
            new0 = row0 * wide(scale0)
            new1 = (row1 - wide(b * inv_a) * row0) * wide(scale1)
            out = jnp.where(rows2 == k, new0, jnp.where(rows2 == k + 1, new1, out))
        A[pl.ds(base, 16), :] = out
        weights = jnp.where(lanes >= base + 16, out[:, :RANK], 0.0)
        A[...] = A[...] - lax.dot_general(
            weights, out, (((0,), (0,)), ((), ())), precision=HIGH, preferred_element_type=F32
        )
        return 0

    lax.fori_loop(0, RANK // 16, body, 0)


def kernel(
    grad, inp, pre, error, w_down, w_up, q_init,
    gdown_out, gup_out, err_out, recv_out,
    G, X, PRE, HID, GP, WD, WU, H, HF, RSA, RSB, C, SB, X2, BK, GD, ACC, GU, OWN, ERR, MRG,
    Q, MB, STACK, MC, LF, A, AP, AR, RR,
    send, recv, send_rank, recv_rank, local,
):
    s = lax.axis_index("section")
    t = lax.axis_index("tensor")
    d = lax.axis_index("dp")
    zl, x, c = t // 8, (t // 2) % 4, t % 2
    xr, xl, xo = (x + 1) % 4, (x + 3) % 4, (x + 2) % 4
    dr, dl, do = (d + 1) % 4, (d + 3) % 4, (d + 2) % 4
    above, below = (s + 1) % 4, (s + 3) % 4
    other_z = (1 - zl) * 8 + x * 2 + c
    sib = {"tensor": zl * 8 + x * 2 + (1 - c)}
    zpeer = {"tensor": other_z}
    right = {"tensor": zl * 8 + xr * 2 + c}
    left = {"tensor": zl * 8 + xl * 2 + c}
    opposite = {"tensor": zl * 8 + xo * 2 + c}
    dpr, dpl = {"dp": dr}, {"dp": dl}
    net = Copies(send, recv)

    def peer(k):
        return (t + k) % 16

    def loop(lo, fn):
        def body(k, _):
            fn(k)
            return 0

        lax.fori_loop(lo, 16, body, 0)

    loads = {}

    def done(name):
        loads[name].wait()


    def load(name, src, dst):
        copy = pltpu.make_async_copy(src, dst, local.at[len(loads)])
        copy.start()
        loads[name] = copy

    def cols(block):
        return pl.ds(pl.multiple_of(block * WIDTH, 128), WIDTH)

    def hail(device):
        pl.semaphore_signal(barrier, inc=1, device_id=device, device_id_type=MESH)

    barrier = pltpu.get_barrier_semaphore()
    for to in (do, dr, dl):
        hail({"dp": to})
        hail({"tensor": other_z, "dp": to})
    loop(1, lambda k: hail({"tensor": peer(k)}))
    loop(0, lambda k: hail({"section": above, "tensor": peer(k)}))
    loop(0, lambda k: hail({"section": below, "tensor": peer(k)}))
    load("G", grad.at[:, cols(d)], G.at[d, zl, x, c])
    load("X", inp.at[:, cols(d)], X.at[d, zl, x, c])
    load("WD", w_down, WD)
    load("PRE", pre, PRE.at[d])
    load("WU", w_up, WU)
    load("OWN", grad, OWN)
    load("ERR", error, ERR)
    load("Q", q_init, Q)
    pl.semaphore_wait(barrier, 53)


    targets = (do, dr, dl, d)

    def scatter(src, dst, k):
        to = targets[k]
        part = dst.at[d, zl, x, c]
        made = [net.start(src.at[:, cols(to)], part, {"tensor": other_z, "dp": to})]
        if k < 3:
            made.append(net.start(src.at[:, cols(to)], part, {"dp": to}))
        return made

    order = (do, dr, dl, d)
    arrive = (0, 2, 1, 3)

    def gather_first(buf, r, copies):
        for copy in copies:
            copy.wait_recv()
        pair = buf.at[r, :, x, c]
        return dict(
            x=[net.start(pair, pair, device) for device in (right, left, opposite)],
            s=[net.start(pair, pair, sib)],
        )

    def gather_second(buf, r, state):
        for copy, at in zip(state["x"], (xl, xr, xo)):
            copy.wait_recv()
            pair = buf.at[r, :, at, c]
            state["s"].append(net.start(pair, pair, sib))

    def gather_last(state):
        for copy in state["s"]:
            copy.wait_recv()

    g_scatter = [scatter(grad, G, 0)]
    done("G")
    g_states = [gather_first(G, order[0], g_scatter[0])]
    g_scatter += [scatter(grad, G, k) for k in (1, 2, 3)]
    for copies in g_scatter:
        for copy in copies:
            copy.wait_send()
    x_scatter = [scatter(inp, X, k) for k in range(4)]
    pre_part = [pre.at[pl.ds(0, 128)], pre.at[pl.ds(128, 128)]]
    pre_to = [PRE.at[d, pl.ds(0, 128)], PRE.at[d, pl.ds(128, 128)]]

    def pre_first():
        return (
            net.start(pre_part[0], pre_to[0], dpr),
            net.start(pre_part[1], pre_to[1], dpl),
        )


    def hidden_part(r, store):
        store(
            lax.dot_general(
                G[r].reshape(GROUP, WIDTH),
                WD[...],
                (((1,), (1,)), ((), ())),
                preferred_element_type=F32,
            )
        )

    def store_bf(k):
        def store(value):
            H[k] = value.astype(BF)

        return store

    def store_own(value):
        HF[...] = value

    top = [pl.ds(0, 64), pl.ds(64, 64)]
    low = [pl.ds(128, 64), pl.ds(192, 64)]
    rsa, early, late = [], [], []
    for k, r in enumerate(order):
        gather_second(G, r, g_states[k])
        if k == 0:
            for n in (1, 2):
                g_states.append(gather_first(G, order[n], g_scatter[arrive[n]]))
            done("WD")
        if k == 2:
            g_states.append(gather_first(G, order[3], g_scatter[arrive[3]]))
        gather_last(g_states[k])
        hidden_part(r, store_own if k == 3 else store_bf(k))
        if k == 0:
            for q in (0, 1):
                rsa.append(
                    (
                        net.start(H.at[0, top[q]], RSA.at[0, top[q]], dpr),
                        net.start(H.at[0, low[q]], RSA.at[1, top[q]], dpl),
                    )
                )
        if k == 1:
            early_r = net.start(H.at[1, low[0]], RSB.at[0, low[0]], dpr)
        if k == 2:
            early.append((early_r, net.start(H.at[2, top[0]], RSB.at[1, top[0]], dpl)))


    def add_rows(k, base, part, q):
        def body(j, _):
            at = pl.ds(pl.multiple_of(base + q * 64 + j * 16, 16), 16)
            at_part = pl.ds(pl.multiple_of(q * 64 + j * 16, 16), 16)
            H[k, at, :] = (H[k, at, :].astype(F32) + RSA[part, at_part, :].astype(F32)).astype(BF)
            return 0

        lax.fori_loop(0, 4, body, 0)

    done("X")
    x_states = [gather_first(X, order[k], x_scatter[arrive[k]]) for k in range(4)]

    for q in (0, 1):
        rsa[q][0].wait_recv()
        add_rows(1, 0, 0, q)
        late_r = net.start(H.at[1, top[q]], RSB.at[0, top[q]], dpr)
        rsa[q][1].wait_recv()
        add_rows(2, 128, 1, q)
        late.append((late_r, net.start(H.at[2, low[q]], RSB.at[1, low[q]], dpl)))
        if q == 0:
            early.append(
                (
                    net.start(H.at[1, low[1]], RSB.at[0, low[1]], dpr),
                    net.start(H.at[2, top[1]], RSB.at[1, top[1]], dpl),
                )
            )

    def own_slope(half, q):
        def body(j, _):
            at = pl.ds(pl.multiple_of(half * 128 + q * 64 + j * 16, 16), 16)
            to = pl.ds(pl.multiple_of(q * 64 + j * 16, 16), 16)
            total = HF[at, :] + RSB[0, at, :].astype(F32) + RSB[1, at, :].astype(F32)
            GP[d, half, to, :] = (total * gelu_slope(PRE[d, at, :].astype(F32))).astype(BF)
            return 0

        lax.fori_loop(0, 4, body, 0)

    done("PRE")
    gp = []
    for q in (0, 1):
        for copy in early[q] + late[q]:
            copy.wait_recv()
        own_slope(0, q)
        own_slope(1, q)
        part = GP.at[d, :, top[q]]
        gp.append((net.start(part, part, dpr), net.start(part, part, dpl)))

    def pass_on(q):
        gp[q][0].wait_recv()
        part = GP.at[dl, 0, top[q]]
        one = net.start(part, part, dpr)
        gp[q][1].wait_recv()
        part = GP.at[dr, 1, top[q]]
        return one, net.start(part, part, dpl)

    def up_part(r):
        def body(j, _):
            at = pl.ds(pl.multiple_of(j * 768, 256), 768)
            value = lax.dot_general(
                GP[r].reshape(GROUP, HIDDEN),
                WU[at, :],
                (((1,), (1,)), ((), ())),
                preferred_element_type=F32,
            )
            C[r, :, :, :, :, at] = value.astype(BF).reshape(2, 4, 2, 16, 768)
            return 0

        lax.fori_loop(0, WIDTH // 768, body, 0)

    def s1(r, st):
        up_part(r)
        st["s"] = net.start(C.at[r, :, :, 1 - c], SB.at[r], sib)

    def s2(r, st):
        st["s"].wait_recv()

        def add(at):
            def body(a, _):
                C[r, a, at, c] = (
                    C[r, a, at, c].astype(F32) + SB[r, a, at].astype(F32)
                ).astype(BF)
                return 0

            lax.fori_loop(0, 2, body, 0)

        st["x"] = []
        for at, slot, device in ((xo, 2, opposite), (xr, 0, right), (xl, 1, left)):
            add(at)
            st["x"].append(net.start(C.at[r, :, at, c], X2.at[r, slot], device))
        add(x)

    def s4(r, st, own=False):
        for copy in st["x"]:
            copy.wait_recv()
        for a in (0, 1):
            C[r, a, x, c] = (
                (C[r, a, x, c].astype(F32) + X2[r, 0, a].astype(F32))
                + (X2[r, 1, a].astype(F32) + X2[r, 2, a].astype(F32))
            ).astype(BF)
        same, across = C.at[r, zl, x, c], C.at[r, 1 - zl, x, c]
        if own:
            st["b"] = [net.start(across, BK.at[d, zl], zpeer)]
            BK[d, zl] = C[d, zl, x, c]
        else:
            st["b"] = [
                net.start(same, BK.at[d, zl], {"dp": r}),
                net.start(across, BK.at[d, zl], {"tensor": other_z, "dp": r}),
            ]

    chain = (d, dl, dr, do)
    st = [dict() for _ in chain]
    for r, state in zip(order, x_states):
        gather_second(X, r, state)
    done("WU")
    s1(chain[0], st[0])
    fwd = [pass_on(0)]
    s2(chain[0], st[0])
    fwd.append(pass_on(1))
    s1(chain[1], st[1])
    s1(chain[2], st[2])
    s4(chain[0], st[0], own=True)
    s2(chain[1], st[1])
    s2(chain[2], st[2])

    def up_grad(lo, hi):
        def body(j, _):
            at = pl.ds(pl.multiple_of(j * 256, 256), 256)
            rows = X[:, :, :, :, :, at].reshape(4 * GROUP, 256)
            value = lax.dot_general(
                rows,
                GP[...].reshape(4 * GROUP, HIDDEN),
                (((0,), (0,)), ((), ())),
                preferred_element_type=F32,
            )
            GU[at, :] = value.astype(BF)
            return 0

        lax.fori_loop(lo, hi, body, 0)

    def activate(r):
        def body(j, _):
            at = pl.ds(pl.multiple_of(j * 16, 16), 16)
            HID[r, at, :] = gelu_value(PRE[r, at, :].astype(F32)).astype(BF)
            return 0

        lax.fori_loop(0, 16, body, 0)

    def down_part(r, at):
        return lax.dot_general(
            HID[r, :, at],
            G[r].reshape(GROUP, WIDTH),
            (((0,), (0,)), ((), ())),
            preferred_element_type=F32,
        )

    def down_first():
        def body(j, _):
            at = pl.ds(pl.multiple_of(j * 256, 256), 256)
            ACC[at, :] = (down_part(d, at) + down_part(dl, at)) + down_part(dr, at)
            return 0

        lax.fori_loop(0, 3, body, 0)

    def down_last():
        def body(j, _):
            at = pl.ds(pl.multiple_of(j * 256, 256), 256)
            GD[at, :] = (ACC[at, :] + down_part(do, at)).astype(BF)
            return 0

        lax.fori_loop(0, 3, body, 0)

    def pre_second():
        pre_a[0].wait_recv()
        part = PRE.at[dl, pl.ds(0, 128)]
        one = net.start(part, part, dpr)
        pre_a[1].wait_recv()
        part = PRE.at[dr, pl.ds(128, 128)]
        return one, net.start(part, part, dpl)

    def pre_third():
        return (
            net.start(pre_part[1], pre_to[1], dpr),
            net.start(pre_part[0], pre_to[0], dpl),
        )

    for pair in fwd:
        for copy in pair:
            copy.wait_recv()
    pre_a = pre_first()
    pre_b = pre_third()
    s1(chain[3], st[3])
    s4(chain[1], st[1])
    s4(chain[2], st[2])
    for state in x_states:
        gather_last(state)
    s2(chain[3], st[3])
    up_grad(0, 6)
    load("GU", GU, gup_out)
    s4(chain[3], st[3])
    activate(d)

    done("OWN")
    done("ERR")
    for k in range(4):
        for copy in st[k]["b"]:
            copy.wait_recv()
    for b in range(4):
        at = pl.ds(b * WIDTH, WIDTH)
        block = BK[b, 0].astype(F32) + BK[b, 1].astype(F32)
        merged = OWN[:, at].astype(F32) + ERR[:, at] + block
        MRG[:, at] = merged
        high = merged.astype(BF)
        STACK[pl.ds(0, 16), at] = high
        STACK[pl.ds(16, 16), at] = (merged - high.astype(F32)).astype(BF)
    done("Q")
    both = jnp.dot(STACK[...], Q[...], preferred_element_type=F32)
    LF[t] = both[:16] + both[16:]

    def rc(src, dst, at, device):
        return pltpu.make_async_remote_copy(
            src_ref=src,
            dst_ref=dst,
            send_sem=send_rank.at[at],
            recv_sem=recv_rank.at[at],
            device_id=device,
            device_id_type=MESH,
        )

    def left_copy(k):
        return rc(LF.at[t], LF.at[t], k, {"tensor": peer(k)})

    def block_copy(k):
        return rc(MB.at[peer(k)], MC.at[t], 16 + k, {"tensor": peer(k)})

    def back_copy(k):
        return rc(AP.at[peer(k)], AR.at[t], 32 + k, {"tensor": peer(k)})

    def relay_copy(k):
        return rc(AP.at[peer(k)], RR.at[t], 48 + k, {"section": below, "tensor": peer(k)})

    loop(1, lambda k: left_copy(k).start())
    for b in range(16):
        MB[b] = STACK[pl.ds(0, 16), pl.ds(b * PIECE, PIECE)]
    loop(1, lambda k: block_copy(k).start())
    MC[t] = MB[t]
    A[:, pl.ds(RANK, RANK)] = (
        lax.broadcasted_iota(jnp.int32, (RANK, RANK), 0)
        == lax.broadcasted_iota(jnp.int32, (RANK, RANK), 1)
    ).astype(F32)
    loop(1, lambda k: left_copy(k).wait_recv())
    pre_f = pre_second()
    all_left = LF[...].reshape(GROUP, RANK)
    A[:, pl.ds(0, RANK)] = lax.dot_general(
        all_left, all_left, (((0,), (0,)), ((), ())), precision=HIGH, preferred_element_type=F32
    )
    factor_inverse(A)
    ortho = lax.dot_general(
        all_left, A[:, pl.ds(RANK, RANK)], (((1,), (1,)), ((), ())),
        precision=HIGH, preferred_element_type=F32,
    ).astype(BF)
    loop(1, lambda k: block_copy(k).wait_recv())
    factor = lax.dot_general(
        MC[...].reshape(GROUP, PIECE), ortho, (((0,), (0,)), ((), ())), preferred_element_type=F32
    ).astype(BF)
    approx = lax.dot_general(
        ortho, factor, (((1,), (1,)), ((), ())), preferred_element_type=F32
    ).astype(BF)
    AP[...] = approx.reshape(16, ROWS, PIECE)
    loop(1, lambda k: back_copy(k).start())
    loop(0, lambda k: relay_copy(k).start())
    AR[t] = AP[t]

    for copy in pre_b:
        copy.wait_recv()
    activate(dl)
    activate(dr)
    down_first()
    loop(1, lambda k: back_copy(k).wait_recv())
    for b in range(16):
        at = pl.ds(b * PIECE, PIECE)
        err_out[:, at] = MRG[:, at] - AR[b].astype(F32)
    loop(0, lambda k: relay_copy(k).wait_recv())
    for b in range(16):
        at = pl.ds(b * PIECE, PIECE)
        recv_out[:, at] = jnp.where(s == 3, jnp.zeros((ROWS, PIECE), BF), RR[b])
    for copy in pre_f:
        copy.wait_recv()
    activate(do)
    down_last()
    load("GD", GD, gdown_out)
    loop(1, lambda k: left_copy(k).wait_send())
    loop(1, lambda k: block_copy(k).wait_send())
    loop(1, lambda k: back_copy(k).wait_send())
    loop(0, lambda k: relay_copy(k).wait_send())
    done("GU")
    done("GD")
    net.finish()


def call(grad, inp, pre, error, w_down, w_up, q):
    vm = pltpu.VMEM
    whole = (4, 2, 4, 2, ROWS, WIDTH)
    any_spec = pl.BlockSpec(memory_space=pl.ANY)
    vm_spec = pl.BlockSpec(memory_space=pltpu.VMEM)
    return pl.pallas_call(
        kernel,
        out_shape=(
            jax.ShapeDtypeStruct((HIDDEN, WIDTH), BF),
            jax.ShapeDtypeStruct((WIDTH, HIDDEN), BF),
            jax.ShapeDtypeStruct((ROWS, MODEL), F32),
            jax.ShapeDtypeStruct((ROWS, MODEL), BF),
        ),
        in_specs=[any_spec] * 7,
        out_specs=(any_spec, any_spec, vm_spec, vm_spec),
        scratch_shapes=[
            vm(whole, BF),
            vm(whole, BF),
            vm((4, GROUP, HIDDEN), BF),
            vm((4, GROUP, HIDDEN), BF),
            vm((4, 2, 128, HIDDEN), BF),
            vm((HIDDEN, WIDTH), BF),
            vm((WIDTH, HIDDEN), BF),
            vm((3, GROUP, HIDDEN), BF),
            vm((GROUP, HIDDEN), F32),
            vm((2, 128, HIDDEN), BF),
            vm((2, GROUP, HIDDEN), BF),
            vm(whole, BF),
            vm((4, 2, 4, ROWS, WIDTH), BF),
            vm((4, 3, 2, ROWS, WIDTH), BF),
            vm((4, 2, ROWS, WIDTH), BF),
            vm((HIDDEN, WIDTH), BF),
            vm((HIDDEN, WIDTH), F32),
            vm((WIDTH, HIDDEN), BF),
            vm((ROWS, MODEL), BF),
            vm((ROWS, MODEL), F32),
            vm((ROWS, MODEL), F32),
            vm((MODEL, RANK), BF),
            vm((16, ROWS, PIECE), BF),
            vm((2 * ROWS, MODEL), BF),
            vm((16, ROWS, PIECE), BF),
            vm((16, ROWS, RANK), F32),
            vm((RANK, 2 * RANK), F32),
            vm((16, ROWS, PIECE), BF),
            vm((16, ROWS, PIECE), BF),
            vm((16, ROWS, PIECE), BF),
            pltpu.SemaphoreType.DMA((140,)),
            pltpu.SemaphoreType.DMA((140,)),
            pltpu.SemaphoreType.DMA((64,)),
            pltpu.SemaphoreType.DMA((64,)),
            pltpu.SemaphoreType.DMA((10,)),
        ],
        compiler_params=pltpu.CompilerParams(
            collective_id=0, has_side_effects=True, vmem_limit_bytes=58 * 2**20
        ),
        name="block",
    )(grad, inp, pre, error, w_down, w_up, q)


def copy_kernel(*refs):
    sem = refs[12]
    pieces = []
    for n in range(4):
        src, dst, held = refs[n], refs[4 + n], refs[8 + n]
        step = src.shape[0] // PARTS[n]
        for k in range(PARTS[n]):
            at = pl.ds(k * step, step)
            to = len(pieces)
            load = pltpu.make_async_copy(src.at[at], held.at[at], sem.at[0, to])
            load.start()
            store = pltpu.make_async_copy(held.at[at], dst.at[at], sem.at[1, to])
            pieces.append((load, store))
    for load, store in pieces:
        load.wait()
        store.start()
    for load, store in pieces:
        store.wait()


def copy_call(values):
    any_spec = pl.BlockSpec(memory_space=pl.ANY)
    return pl.pallas_call(
        copy_kernel,
        out_shape=tuple(jax.ShapeDtypeStruct(v.shape, v.dtype) for v in values),
        in_specs=[any_spec] * 4,
        out_specs=(any_spec,) * 4,
        scratch_shapes=[pltpu.VMEM(v.shape, v.dtype) for v in values]
        + [pltpu.SemaphoreType.DMA((2, sum(PARTS)))],
        compiler_params=pltpu.CompilerParams(vmem_limit_bytes=60 * 2**20),
        name="deliver",
    )(*values)


def shards(grad_out, saved_input, pre_act, error, w_up, w_down, q_init):
    grad_down, grad_up, new_error, received = call(
        grad_out[0, 0], saved_input[0, 0], pre_act[0, 0], error[0, 0], w_down[0], w_up[0], q_init[0]
    )
    grad_down, grad_up, new_error, received = copy_call((grad_down, grad_up, new_error, received))
    return (grad_up[None], grad_down[None], new_error[None, None], received[None, None])


def solution(mesh):
    in_specs = (
        P("section", "dp", "tensor", None),
        P("section", "dp", "tensor", None),
        P("section", "dp", None, "tensor"),
        P("section", "dp", "tensor", None),
        P("section", "dp", "tensor"),
        P("section", "tensor", "dp"),
        P("section", None, None),
    )
    out_specs = (
        P("section", "dp", "tensor"),
        P("section", "tensor", "dp"),
        P("section", "dp", "tensor", None),
        P("section", "dp", "tensor", None),
    )
    return jax.shard_map(shards, mesh=mesh, in_specs=in_specs, out_specs=out_specs, check_vma=False)
```

```python
import jax
import jax.numpy as jnp
from jax import lax
from jax.experimental import pallas as pl
from jax.experimental.pallas import tpu as pltpu
from jax.sharding import PartitionSpec as P

BF, F32 = jnp.bfloat16, jnp.float32
MESH = pl.DeviceIdType.MESH
ROWS = 16
GROUP = 256
WIDTH = 1536
HIDDEN = 768
MODEL = 6144
RANK = 128
PIECE = 384
PARTS = (4, 4, 1, 1)
K0 = 0.7978845608
K1 = 0.044715
HIGH = lax.Precision.HIGHEST


class Tracked:
    def __init__(self, copy):
        self.copy, self.sent, self.received = copy, False, False

    def start(self):
        self.copy.start()

    def wait_send(self):
        self.copy.wait_send()
        self.sent = True

    def wait_recv(self):
        self.copy.wait_recv()
        self.received = True


class Copies:
    def __init__(self, send, recv):
        self.send, self.recv, self.count, self.made = send, recv, 0, []

    def new(self, src, dst, device):
        at = self.count
        self.count += 1
        copy = pltpu.make_async_remote_copy(
            src_ref=src,
            dst_ref=dst,
            send_sem=self.send.at[at],
            recv_sem=self.recv.at[at],
            device_id=device,
            device_id_type=MESH,
        )
        copy = Tracked(copy)
        self.made.append(copy)
        return copy

    def start(self, src, dst, device):
        copy = self.new(src, dst, device)
        copy.start()
        return copy

    def finish(self):
        for copy in self.made:
            if not copy.sent:
                copy.wait_send()


def add_slabs(dst, src, count):
    def body(j, _):
        dst[j] = (dst[j].astype(F32) + src[j].astype(F32)).astype(BF)
        return 0

    lax.fori_loop(0, count, body, 0)


def gelu_value(v):
    return 0.5 * v * (1.0 + jnp.tanh(K0 * (v + K1 * (v * v * v))))


def gelu_slope(v):
    square = v * v
    th = jnp.tanh(K0 * (v + K1 * (square * v)))
    return 0.5 * (1.0 + th) + (0.5 * K0) * v * (1.0 - th * th) * (1.0 + (3.0 * K1) * square)


def factor_inverse(A):
    rows = lax.broadcasted_iota(jnp.int32, (16, RANK), 0)
    lanes = lax.broadcasted_iota(jnp.int32, (16, RANK), 1)
    rows2 = lax.broadcasted_iota(jnp.int32, (16, 2 * RANK), 0)

    def wide(value):
        return jnp.concatenate([value, value], axis=1)

    def body(p, _):
        base = pl.multiple_of(p * 16, 16)
        panel = A[pl.ds(base, 16), :]
        gram = panel[:, :RANK]
        cols = [
            jnp.broadcast_to(
                jnp.sum(jnp.where(lanes == base + j, gram, 0.0), axis=1, keepdims=True), (16, RANK)
            )
            for j in range(16)
        ]
        out = jnp.zeros((16, 2 * RANK), F32)
        for k in range(0, 16, 2):
            one, two = cols[k], cols[k + 1]
            a, b, e = one[k : k + 1], two[k : k + 1], two[k + 1 : k + 2]
            det = a * e - b * b
            inv = 1.0 / det
            below = rows >= k + 2
            m0 = jnp.where(below, (e * one - b * two) * inv, 0.0)
            m1 = jnp.where(below, (a * two - b * one) * inv, 0.0)
            for j in range(k + 2, 16):
                cols[j] = cols[j] - (m0 * cols[j][k : k + 1] + m1 * cols[j][k + 1 : k + 2])
            row0, row1 = panel[k : k + 1], panel[k + 1 : k + 2]
            panel = panel - (wide(m0) * row0 + wide(m1) * row1)
            inv_a = 1.0 / a
            scale0 = lax.rsqrt(a)
            scale1 = lax.rsqrt(det * inv_a)
            new0 = row0 * wide(scale0)
            new1 = (row1 - wide(b * inv_a) * row0) * wide(scale1)
            out = jnp.where(rows2 == k, new0, jnp.where(rows2 == k + 1, new1, out))
        A[pl.ds(base, 16), :] = out
        weights = jnp.where(lanes >= base + 16, out[:, :RANK], 0.0)
        A[...] = A[...] - lax.dot_general(
            weights, out, (((0,), (0,)), ((), ())), precision=HIGH, preferred_element_type=F32
        )
        return 0

    lax.fori_loop(0, RANK // 16, body, 0)


def kernel(
    grad, inp, pre, error, w_down, w_up, q_init,
    gdown_out, gup_out, err_out, recv_out,
    G, X, PRE, HID, GP, WD, WU, H, HF, RSA, RSB, C, SB, X2, BK, GD, ACC, GU, OWN, ERR, MRG,
    Q, MB, STACK, MC, LF, A, AP, AR, RR,
    send, recv, send_rank, recv_rank, local,
):
    s = lax.axis_index("section")
    t = lax.axis_index("tensor")
    d = lax.axis_index("dp")
    zl, x, c = t // 8, (t // 2) % 4, t % 2
    xr, xl, xo = (x + 1) % 4, (x + 3) % 4, (x + 2) % 4
    dr, dl, do = (d + 1) % 4, (d + 3) % 4, (d + 2) % 4
    above, below = (s + 1) % 4, (s + 3) % 4
    other_z = (1 - zl) * 8 + x * 2 + c
    sib = {"tensor": zl * 8 + x * 2 + (1 - c)}
    zpeer = {"tensor": other_z}
    right = {"tensor": zl * 8 + xr * 2 + c}
    left = {"tensor": zl * 8 + xl * 2 + c}
    opposite = {"tensor": zl * 8 + xo * 2 + c}
    dpr, dpl = {"dp": dr}, {"dp": dl}
    net = Copies(send, recv)

    def peer(k):
        return (t + k) % 16

    def loop(lo, fn):
        def body(k, _):
            fn(k)
            return 0

        lax.fori_loop(lo, 16, body, 0)

    loads = {}

    def done(name):
        loads[name].wait()


    def load(name, src, dst):
        copy = pltpu.make_async_copy(src, dst, local.at[len(loads)])
        copy.start()
        loads[name] = copy

    def cols(block):
        return pl.ds(pl.multiple_of(block * WIDTH, 128), WIDTH)

    def hail(device):
        pl.semaphore_signal(barrier, inc=1, device_id=device, device_id_type=MESH)

    barrier = pltpu.get_barrier_semaphore()
    for to in (do, dr, dl):
        hail({"dp": to})
        hail({"tensor": other_z, "dp": to})
    loop(1, lambda k: hail({"tensor": peer(k)}))
    loop(0, lambda k: hail({"section": above, "tensor": peer(k)}))
    loop(0, lambda k: hail({"section": below, "tensor": peer(k)}))
    load("G", grad.at[:, cols(d)], G.at[d, zl, x, c])
    load("X", inp.at[:, cols(d)], X.at[d, zl, x, c])
    load("WD", w_down, WD)
    load("PRE", pre, PRE.at[d])
    load("WU", w_up, WU)
    load("OWN", grad, OWN)
    load("ERR", error, ERR)
    load("Q", q_init, Q)
    pl.semaphore_wait(barrier, 53)


    targets = (do, dr, dl, d)

    def scatter(src, dst, k):
        to = targets[k]
        part = dst.at[d, zl, x, c]
        made = [net.start(src.at[:, cols(to)], part, {"tensor": other_z, "dp": to})]
        if k < 3:
            made.append(net.start(src.at[:, cols(to)], part, {"dp": to}))
        return made

    order = (do, dr, dl, d)
    arrive = (0, 2, 1, 3)

    def gather_first(buf, r, copies):
        for copy in copies:
            copy.wait_recv()
        pair = buf.at[r, :, x, c]
        return dict(
            x=[net.start(pair, pair, device) for device in (right, left, opposite)],
            s=[net.start(pair, pair, sib)],
        )

    def gather_second(buf, r, state):
        for copy, at in zip(state["x"], (xl, xr, xo)):
            copy.wait_recv()
            pair = buf.at[r, :, at, c]
            state["s"].append(net.start(pair, pair, sib))

    def gather_last(state):
        for copy in state["s"]:
            copy.wait_recv()

    g_scatter = [scatter(grad, G, 0)]
    done("G")
    g_states = [gather_first(G, order[0], g_scatter[0])]
    g_scatter += [scatter(grad, G, k) for k in (1, 2, 3)]
    for copies in g_scatter:
        for copy in copies:
            copy.wait_send()
    x_scatter = [scatter(inp, X, k) for k in range(4)]
    pre_part = [pre.at[pl.ds(0, 128)], pre.at[pl.ds(128, 128)]]
    pre_to = [PRE.at[d, pl.ds(0, 128)], PRE.at[d, pl.ds(128, 128)]]

    def pre_first():
        return (
            net.start(pre_part[0], pre_to[0], dpr),
            net.start(pre_part[1], pre_to[1], dpl),
        )


    def hidden_part(r, store):
        store(
            lax.dot_general(
                G[r].reshape(GROUP, WIDTH),
                WD[...],
                (((1,), (1,)), ((), ())),
                preferred_element_type=F32,
            )
        )

    def store_bf(k):
        def store(value):
            H[k] = value.astype(BF)

        return store

    def store_own(value):
        HF[...] = value

    top = [pl.ds(0, 64), pl.ds(64, 64)]
    low = [pl.ds(128, 64), pl.ds(192, 64)]
    rsa, early, late = [], [], []
    for k, r in enumerate(order):
        gather_second(G, r, g_states[k])
        if k == 0:
            for n in (1, 2):
                g_states.append(gather_first(G, order[n], g_scatter[arrive[n]]))
            done("WD")
        if k == 2:
            g_states.append(gather_first(G, order[3], g_scatter[arrive[3]]))
        gather_last(g_states[k])
        hidden_part(r, store_own if k == 3 else store_bf(k))
        if k == 0:
            for q in (0, 1):
                rsa.append(
                    (
                        net.start(H.at[0, top[q]], RSA.at[0, top[q]], dpr),
                        net.start(H.at[0, low[q]], RSA.at[1, top[q]], dpl),
                    )
                )
        if k == 1:
            early_r = net.start(H.at[1, low[0]], RSB.at[0, low[0]], dpr)
        if k == 2:
            early.append((early_r, net.start(H.at[2, top[0]], RSB.at[1, top[0]], dpl)))


    def add_rows(k, base, part, q):
        def body(j, _):
            at = pl.ds(pl.multiple_of(base + q * 64 + j * 16, 16), 16)
            at_part = pl.ds(pl.multiple_of(q * 64 + j * 16, 16), 16)
            H[k, at, :] = (H[k, at, :].astype(F32) + RSA[part, at_part, :].astype(F32)).astype(BF)
            return 0

        lax.fori_loop(0, 4, body, 0)

    done("X")
    x_states = [gather_first(X, order[k], x_scatter[arrive[k]]) for k in range(4)]

    for q in (0, 1):
        rsa[q][0].wait_recv()
        add_rows(1, 0, 0, q)
        late_r = net.start(H.at[1, top[q]], RSB.at[0, top[q]], dpr)
        rsa[q][1].wait_recv()
        add_rows(2, 128, 1, q)
        late.append((late_r, net.start(H.at[2, low[q]], RSB.at[1, low[q]], dpl)))
        if q == 0:
            early.append(
                (
                    net.start(H.at[1, low[1]], RSB.at[0, low[1]], dpr),
                    net.start(H.at[2, top[1]], RSB.at[1, top[1]], dpl),
                )
            )

    def own_slope(half, q):
        def body(j, _):
            at = pl.ds(pl.multiple_of(half * 128 + q * 64 + j * 16, 16), 16)
            to = pl.ds(pl.multiple_of(q * 64 + j * 16, 16), 16)
            total = HF[at, :] + RSB[0, at, :].astype(F32) + RSB[1, at, :].astype(F32)
            GP[d, half, to, :] = (total * gelu_slope(PRE[d, at, :].astype(F32))).astype(BF)
            return 0

        lax.fori_loop(0, 4, body, 0)

    done("PRE")
    gp = []
    for q in (0, 1):
        for copy in early[q] + late[q]:
            copy.wait_recv()
        own_slope(0, q)
        own_slope(1, q)
        part = GP.at[d, :, top[q]]
        gp.append((net.start(part, part, dpr), net.start(part, part, dpl)))

    def pass_on(q):
        gp[q][0].wait_recv()
        part = GP.at[dl, 0, top[q]]
        one = net.start(part, part, dpr)
        gp[q][1].wait_recv()
        part = GP.at[dr, 1, top[q]]
        return one, net.start(part, part, dpl)

    def up_part(r):
        def body(j, _):
            at = pl.ds(pl.multiple_of(j * 768, 256), 768)
            value = lax.dot_general(
                GP[r].reshape(GROUP, HIDDEN),
                WU[at, :],
                (((1,), (1,)), ((), ())),
                preferred_element_type=F32,
            )
            C[r, :, :, :, :, at] = value.astype(BF).reshape(2, 4, 2, 16, 768)
            return 0

        lax.fori_loop(0, WIDTH // 768, body, 0)

    def s1(r, st):
        up_part(r)
        st["s"] = net.start(C.at[r, :, :, 1 - c], SB.at[r], sib)

    def s2(r, st):
        st["s"].wait_recv()

        def add(at):
            def body(a, _):
                C[r, a, at, c] = (
                    C[r, a, at, c].astype(F32) + SB[r, a, at].astype(F32)
                ).astype(BF)
                return 0

            lax.fori_loop(0, 2, body, 0)

        st["x"] = []
        for at, slot, device in ((xo, 2, opposite), (xr, 0, right), (xl, 1, left)):
            add(at)
            st["x"].append(net.start(C.at[r, :, at, c], X2.at[r, slot], device))
        add(x)

    def s4(r, st, own=False):
        for copy in st["x"]:
            copy.wait_recv()
        for a in (0, 1):
            C[r, a, x, c] = (
                (C[r, a, x, c].astype(F32) + X2[r, 0, a].astype(F32))
                + (X2[r, 1, a].astype(F32) + X2[r, 2, a].astype(F32))
            ).astype(BF)
        same, across = C.at[r, zl, x, c], C.at[r, 1 - zl, x, c]
        if own:
            st["b"] = [net.start(across, BK.at[d, zl], zpeer)]
            BK[d, zl] = C[d, zl, x, c]
        else:
            st["b"] = [
                net.start(same, BK.at[d, zl], {"dp": r}),
                net.start(across, BK.at[d, zl], {"tensor": other_z, "dp": r}),
            ]

    chain = (d, dl, dr, do)
    st = [dict() for _ in chain]
    for r, state in zip(order, x_states):
        gather_second(X, r, state)
    done("WU")
    s1(chain[0], st[0])
    fwd = [pass_on(0)]
    s2(chain[0], st[0])
    fwd.append(pass_on(1))
    s1(chain[1], st[1])
    s1(chain[2], st[2])
    s2(chain[1], st[1])
    s2(chain[2], st[2])
    s4(chain[0], st[0], own=True)

    def up_grad(lo, hi):
        def body(j, _):
            at = pl.ds(pl.multiple_of(j * 256, 256), 256)
            rows = X[:, :, :, :, :, at].reshape(4 * GROUP, 256)
            value = lax.dot_general(
                rows,
                GP[...].reshape(4 * GROUP, HIDDEN),
                (((0,), (0,)), ((), ())),
                preferred_element_type=F32,
            )
            GU[at, :] = value.astype(BF)
            return 0

        lax.fori_loop(lo, hi, body, 0)

    def activate(r):
        def body(j, _):
            at = pl.ds(pl.multiple_of(j * 16, 16), 16)
            HID[r, at, :] = gelu_value(PRE[r, at, :].astype(F32)).astype(BF)
            return 0

        lax.fori_loop(0, 16, body, 0)

    def down_part(r, at):
        return lax.dot_general(
            HID[r, :, at],
            G[r].reshape(GROUP, WIDTH),
            (((0,), (0,)), ((), ())),
            preferred_element_type=F32,
        )

    def down_first():
        def body(j, _):
            at = pl.ds(pl.multiple_of(j * 256, 256), 256)
            ACC[at, :] = (down_part(d, at) + down_part(dl, at)) + down_part(dr, at)
            return 0

        lax.fori_loop(0, 3, body, 0)

    def down_last():
        for j in range(3):
            at = pl.ds(j * 256, 256)
            GD[at, :] = (ACC[at, :] + down_part(do, at)).astype(BF)
            load(f"GD{j}", GD.at[at], gdown_out.at[at])

    def pre_second():
        pre_a[0].wait_recv()
        part = PRE.at[dl, pl.ds(0, 128)]
        one = net.start(part, part, dpr)
        pre_a[1].wait_recv()
        part = PRE.at[dr, pl.ds(128, 128)]
        return one, net.start(part, part, dpl)

    def pre_third():
        return (
            net.start(pre_part[1], pre_to[1], dpr),
            net.start(pre_part[0], pre_to[0], dpl),
        )

    for pair in fwd:
        for copy in pair:
            copy.wait_recv()
    pre_a = pre_first()
    pre_b = pre_third()
    s1(chain[3], st[3])
    for state in x_states:
        gather_last(state)
    s2(chain[3], st[3])
    s4(chain[1], st[1])
    s4(chain[2], st[2])
    up_grad(0, 6)
    load("GU", GU, gup_out)
    s4(chain[3], st[3])
    activate(d)

    done("OWN")
    done("ERR")
    for k in range(4):
        for copy in st[k]["b"]:
            copy.wait_recv()
    for b in range(4):
        at = pl.ds(b * WIDTH, WIDTH)
        block = BK[b, 0].astype(F32) + BK[b, 1].astype(F32)
        merged = OWN[:, at].astype(F32) + ERR[:, at] + block
        MRG[:, at] = merged
        high = merged.astype(BF)
        STACK[pl.ds(0, 16), at] = high
        STACK[pl.ds(16, 16), at] = (merged - high.astype(F32)).astype(BF)
    done("Q")
    both = jnp.dot(STACK[...], Q[...], preferred_element_type=F32)
    LF[t] = both[:16] + both[16:]

    def rc(src, dst, at, device):
        return pltpu.make_async_remote_copy(
            src_ref=src,
            dst_ref=dst,
            send_sem=send_rank.at[at],
            recv_sem=recv_rank.at[at],
            device_id=device,
            device_id_type=MESH,
        )

    def left_copy(k):
        return rc(LF.at[t], LF.at[t], k, {"tensor": peer(k)})

    def block_copy(k):
        return rc(MB.at[peer(k)], MC.at[t], 16 + k, {"tensor": peer(k)})

    def back_copy(k):
        return rc(AP.at[peer(k)], AR.at[t], 32 + k, {"tensor": peer(k)})

    def relay_copy(k):
        return rc(AP.at[peer(k)], RR.at[t], 48 + k, {"section": below, "tensor": peer(k)})

    loop(1, lambda k: left_copy(k).start())
    for b in range(16):
        MB[b] = STACK[pl.ds(0, 16), pl.ds(b * PIECE, PIECE)]
    loop(1, lambda k: block_copy(k).start())
    MC[t] = MB[t]
    A[:, pl.ds(RANK, RANK)] = (
        lax.broadcasted_iota(jnp.int32, (RANK, RANK), 0)
        == lax.broadcasted_iota(jnp.int32, (RANK, RANK), 1)
    ).astype(F32)
    loop(1, lambda k: left_copy(k).wait_recv())
    pre_f = pre_second()
    all_left = LF[...].reshape(GROUP, RANK)
    A[:, pl.ds(0, RANK)] = lax.dot_general(
        all_left, all_left, (((0,), (0,)), ((), ())), precision=HIGH, preferred_element_type=F32
    )
    factor_inverse(A)
    ortho = lax.dot_general(
        all_left, A[:, pl.ds(RANK, RANK)], (((1,), (1,)), ((), ())),
        precision=HIGH, preferred_element_type=F32,
    ).astype(BF)
    loop(1, lambda k: block_copy(k).wait_recv())
    factor = lax.dot_general(
        MC[...].reshape(GROUP, PIECE), ortho, (((0,), (0,)), ((), ())), preferred_element_type=F32
    ).astype(BF)
    approx = lax.dot_general(
        ortho, factor, (((1,), (1,)), ((), ())), preferred_element_type=F32
    ).astype(BF)
    AP[...] = approx.reshape(16, ROWS, PIECE)
    loop(1, lambda k: back_copy(k).start())
    loop(0, lambda k: relay_copy(k).start())
    AR[t] = AP[t]

    for copy in pre_b:
        copy.wait_recv()
    activate(dl)
    activate(dr)
    down_first()
    loop(1, lambda k: back_copy(k).wait_recv())
    for b in range(16):
        at = pl.ds(b * PIECE, PIECE)
        err_out[:, at] = MRG[:, at] - AR[b].astype(F32)
    loop(0, lambda k: relay_copy(k).wait_recv())
    for b in range(16):
        at = pl.ds(b * PIECE, PIECE)
        recv_out[:, at] = jnp.where(s == 3, jnp.zeros((ROWS, PIECE), BF), RR[b])
    for copy in pre_f:
        copy.wait_recv()
    activate(do)
    down_last()
    loop(1, lambda k: left_copy(k).wait_send())
    loop(1, lambda k: block_copy(k).wait_send())
    loop(1, lambda k: back_copy(k).wait_send())
    loop(0, lambda k: relay_copy(k).wait_send())
    done("GU")
    for j in range(3):
        done(f"GD{j}")
    net.finish()


def call(grad, inp, pre, error, w_down, w_up, q):
    vm = pltpu.VMEM
    whole = (4, 2, 4, 2, ROWS, WIDTH)
    any_spec = pl.BlockSpec(memory_space=pl.ANY)
    vm_spec = pl.BlockSpec(memory_space=pltpu.VMEM)
    return pl.pallas_call(
        kernel,
        out_shape=(
            jax.ShapeDtypeStruct((HIDDEN, WIDTH), BF),
            jax.ShapeDtypeStruct((WIDTH, HIDDEN), BF),
            jax.ShapeDtypeStruct((ROWS, MODEL), F32),
            jax.ShapeDtypeStruct((ROWS, MODEL), BF),
        ),
        in_specs=[any_spec] * 7,
        out_specs=(any_spec, any_spec, vm_spec, vm_spec),
        scratch_shapes=[
            vm(whole, BF),
            vm(whole, BF),
            vm((4, GROUP, HIDDEN), BF),
            vm((4, GROUP, HIDDEN), BF),
            vm((4, 2, 128, HIDDEN), BF),
            vm((HIDDEN, WIDTH), BF),
            vm((WIDTH, HIDDEN), BF),
            vm((3, GROUP, HIDDEN), BF),
            vm((GROUP, HIDDEN), F32),
            vm((2, 128, HIDDEN), BF),
            vm((2, GROUP, HIDDEN), BF),
            vm(whole, BF),
            vm((4, 2, 4, ROWS, WIDTH), BF),
            vm((4, 3, 2, ROWS, WIDTH), BF),
            vm((4, 2, ROWS, WIDTH), BF),
            vm((HIDDEN, WIDTH), BF),
            vm((HIDDEN, WIDTH), F32),
            vm((WIDTH, HIDDEN), BF),
            vm((ROWS, MODEL), BF),
            vm((ROWS, MODEL), F32),
            vm((ROWS, MODEL), F32),
            vm((MODEL, RANK), BF),
            vm((16, ROWS, PIECE), BF),
            vm((2 * ROWS, MODEL), BF),
            vm((16, ROWS, PIECE), BF),
            vm((16, ROWS, RANK), F32),
            vm((RANK, 2 * RANK), F32),
            vm((16, ROWS, PIECE), BF),
            vm((16, ROWS, PIECE), BF),
            vm((16, ROWS, PIECE), BF),
            pltpu.SemaphoreType.DMA((140,)),
            pltpu.SemaphoreType.DMA((140,)),
            pltpu.SemaphoreType.DMA((64,)),
            pltpu.SemaphoreType.DMA((64,)),
            pltpu.SemaphoreType.DMA((12,)),
        ],
        compiler_params=pltpu.CompilerParams(
            collective_id=0, has_side_effects=True, vmem_limit_bytes=58 * 2**20
        ),
        name="block",
    )(grad, inp, pre, error, w_down, w_up, q)


def copy_kernel(*refs):
    sem = refs[12]
    pieces = []
    for n in range(4):
        src, dst, held = refs[n], refs[4 + n], refs[8 + n]
        step = src.shape[0] // PARTS[n]
        for k in range(PARTS[n]):
            at = pl.ds(k * step, step)
            to = len(pieces)
            load = pltpu.make_async_copy(src.at[at], held.at[at], sem.at[0, to])
            load.start()
            store = pltpu.make_async_copy(held.at[at], dst.at[at], sem.at[1, to])
            pieces.append((load, store))
    for load, store in pieces:
        load.wait()
        store.start()
    for load, store in pieces:
        store.wait()


def copy_call(values):
    any_spec = pl.BlockSpec(memory_space=pl.ANY)
    return pl.pallas_call(
        copy_kernel,
        out_shape=tuple(jax.ShapeDtypeStruct(v.shape, v.dtype) for v in values),
        in_specs=[any_spec] * 4,
        out_specs=(any_spec,) * 4,
        scratch_shapes=[pltpu.VMEM(v.shape, v.dtype) for v in values]
        + [pltpu.SemaphoreType.DMA((2, sum(PARTS)))],
        compiler_params=pltpu.CompilerParams(vmem_limit_bytes=60 * 2**20),
        name="deliver",
    )(*values)


def shards(grad_out, saved_input, pre_act, error, w_up, w_down, q_init):
    grad_down, grad_up, new_error, received = call(
        grad_out[0, 0], saved_input[0, 0], pre_act[0, 0], error[0, 0], w_down[0], w_up[0], q_init[0]
    )
    grad_down, grad_up, new_error, received = copy_call((grad_down, grad_up, new_error, received))
    return (grad_up[None], grad_down[None], new_error[None, None], received[None, None])


def solution(mesh):
    in_specs = (
        P("section", "dp", "tensor", None),
        P("section", "dp", "tensor", None),
        P("section", "dp", None, "tensor"),
        P("section", "dp", "tensor", None),
        P("section", "dp", "tensor"),
        P("section", "tensor", "dp"),
        P("section", None, None),
    )
    out_specs = (
        P("section", "dp", "tensor"),
        P("section", "tensor", "dp"),
        P("section", "dp", "tensor", None),
        P("section", "dp", "tensor", None),
    )
    return jax.shard_map(shards, mesh=mesh, in_specs=in_specs, out_specs=out_specs, check_vma=False)
```
